256 devices in a mesh: row: 16 (over y, x), col: 16 (over z, core).
Axes of the slice: x: 4, y: 4, z: 8, core: 2. Of those that a mesh axis runs over, the one named last changes fastest.
Arguments:
- tensor: float32 [2, 16384, 16384], P(None, 'row', 'col'), may hold values from -6 to 6
- second: float32 [16384, 64], P(('col', 'row')), may hold values from -0.05 to 0.05
- third: float32 [2, 64], replicated, may hold values from 0.5 to 2
Outputs:
- factor: float32 [16384, 64], P(('row', 'col'))
The draws below stay inside these ranges and needn't reach their ends.
All inputs are finite; a program needn't handle non-finite values.
Results may differ from the reference program's by a relative error of at most 0.00016.
Values sent between devices are 32-bit elements; how exact they have to be, the bound alone decides.
No kernel may reach another device: no remote copies, remote signals or barrier semaphores. Data moves between devices by JAX's collectives and lax.ppermute only.
A program may use at most 64 MiB of HBM per device.

```python
import math
import jax
import jax.numpy as jnp
from jax import lax

I = 16384
J = 16384
K = 2
R = 64


def draw_second(key, part):
    key = jax.random.fold_in(key, 7)
    first, shared, gains = jax.random.split(key, 3)
    column_gain = jax.random.uniform(gains, (1, R), jnp.float32, 0.5, 1.5)
    noise = jnp.clip(jax.random.normal(first, (J, R), jnp.float32), -4.0, 4.0)
    common = jnp.clip(jax.random.normal(shared, (J, 1), jnp.float32), -4.0, 4.0)
    return (noise + 0.8 * common * column_gain) * 0.005


def raised(array, key, source, target, parts, factor):
    owner, partner = [(jnp.arange(array.shape[dim]) // (array.shape[dim] // parts)).reshape([-1 if axis == dim else 1 for axis in range(array.ndim)]) for dim in (source, target)]
    chosen = jax.random.permutation(key, parts)[partner]
    strong = (owner == chosen) | (owner == (partner + parts // 2) % parts)
    return jnp.where(strong, factor * array, array)


def level_of(own_key, shape, cuts, low, high):
    loudness = 1.0
    for dim, parts in cuts:
        steps = jax.random.uniform(jax.random.fold_in(jax.random.fold_in(own_key, 6), dim), (parts,), jnp.float32, low / len(cuts), high / len(cuts))
        loudness = loudness * jnp.repeat(jnp.exp(steps), shape[dim] // parts).reshape((-1,) + (1,) * (len(shape) - 1 - dim))
    return loudness


def noise_with(rng, dims, deviation, bound, pieces, heavy, dtype=jnp.bfloat16):
    array = deviation * jax.random.normal(rng, dims, jnp.float32)
    if pieces:
        array = array * level_of(rng, dims, pieces, -0.22, 0.18)
    return jnp.clip(raised(array, jax.random.fold_in(rng, 3), *heavy), -bound, bound).astype(dtype)


def setup_inputs(seed: int = 0) -> dict:
    keys = jax.random.split(jax.random.key(seed), 4)
    return {
        "tensor": noise_with(keys[0], (K, I, J), 1.0, 6.0, ((1, 16), (2, 16)), (2, 1, 16, 2.0), jnp.float32),
        "second": draw_second(jax.random.fold_in(keys[3], 71), 0),
        "third": jnp.clip(jnp.exp(jax.random.uniform(keys[2], (K, R), jnp.float32, math.log(0.5), math.log(2.0))), 0.5, 2.0),
    }


def reference(tensor, second, third):

    def one_slice(total, index):
        weighted = second * third[index][None, :]
        part = jnp.dot(tensor[index].astype(jnp.float32), weighted.astype(jnp.float32), preferred_element_type=jnp.float32, precision=lax.Precision.HIGHEST)
        return (total + part, None)
    mttkrp, _ = lax.scan(one_slice, jnp.zeros((I, R), jnp.float32), jnp.arange(K))
    gram_second = jnp.dot(second.T.astype(jnp.float32), second.astype(jnp.float32), preferred_element_type=jnp.float32, precision=lax.Precision.HIGHEST)
    gram_third = jnp.dot(third.T.astype(jnp.float32), third.astype(jnp.float32), preferred_element_type=jnp.float32, precision=lax.Precision.HIGHEST)
    gram = gram_second * gram_third
    lower = jnp.linalg.cholesky(gram)
    solved = jax.scipy.linalg.cho_solve((lower, True), mttkrp.T)
    return solved.T
```

```python
import jax
import jax.numpy as jnp
from jax import lax
from jax.sharding import PartitionSpec as P


def body(tensor, second, third):
    rank = second.shape[1]
    rows = lax.axis_size("row")
    cols = lax.axis_size("col")
    copies = jnp.broadcast_to(second[None], (rows,) + second.shape)
    block = lax.all_to_all(copies, "row", 0, 0).reshape(-1, rank)
    weighted = block[None, :, :] * third[:, None, :]
    local_gram = jnp.dot(
        block.T, block, preferred_element_type=jnp.float32, precision=lax.Precision.HIGHEST
    )
    partial = jnp.einsum(
        "kij,kjr->ir",
        tensor,
        weighted,
        preferred_element_type=jnp.float32,
        precision=lax.Precision.HIGH,
    )
    parts = partial.reshape(cols, -1, rank)
    share = parts.shape[1]
    grams = jnp.broadcast_to(local_gram[None], (cols, rank, rank))
    sent = jnp.concatenate([parts, grams], axis=1)
    got = lax.all_to_all(sent, "col", 0, 0).sum(0)
    mine = got[:share]
    gram_third = jnp.dot(
        third.T, third, preferred_element_type=jnp.float32, precision=lax.Precision.HIGHEST
    )
    gram = got[share:] * gram_third
    lower = jnp.linalg.cholesky(gram)
    return jax.scipy.linalg.cho_solve((lower, True), mine.T).T


def solution(mesh):
    in_specs = (P(None, "row", "col"), P(("col", "row"), None), P())
    out_specs = P(("row", "col"), None)
    return jax.shard_map(body, mesh=mesh, in_specs=in_specs, out_specs=out_specs, check_vma=False)
```

```python
import jax
import jax.numpy as jnp
from jax import lax
from jax.experimental import pallas as pl
from jax.experimental.pallas import tpu as pltpu
from jax.sharding import PartitionSpec as P

F32 = jnp.float32
BF16 = jnp.bfloat16
RANK = 64
LANES = 128
HALF = 32
STRIP = 8


def vmem():
    return pl.BlockSpec(memory_space=pltpu.VMEM)


def pack_kernel(second_ref, out_ref):
    packed = jnp.concatenate([second_ref[:HALF, :], second_ref[HALF:, :]], axis=1)
    for peer in range(out_ref.shape[0]):
        out_ref[peer] = packed


def swap(x):
    return pltpu.roll(x, RANK, 1)


def product_kernel(tensor_ref, rows_ref, third_ref, out_ref, held, weights, sems):
    slices, own, inner = tensor_ref.shape
    peers = rows_ref.shape[0]
    targets = out_ref.shape[0]
    tile = own // sems.shape[0]
    copies = []
    for t in range(sems.shape[0]):
        part = pl.ds(t * tile, tile)
        copy = pltpu.make_async_copy(tensor_ref.at[:, part], held.at[:, part], sems.at[t])
        copy.start()
        copies.append(copy)

    left = lax.broadcasted_iota(jnp.int32, (HALF, LANES), 1) < RANK
    third = third_ref[...]
    scale = jnp.concatenate([third, third], axis=1)
    for peer in range(peers):
        here = rows_ref[peer]
        there = swap(here)
        for k in range(slices):
            a = here * scale[k : k + 1, :]
            b = there * scale[k : k + 1, :]
            a_hi = a.astype(BF16).astype(F32)
            b_hi = b.astype(BF16).astype(F32)
            first = jnp.where(left, a_hi, b - b_hi)
            other = jnp.where(left, b_hi, a - a_hi)
            base = peer * RANK
            weights[k, base : base + HALF, :] = first.astype(BF16)
            weights[k, base + HALF : base + RANK, :] = other.astype(BF16)

    share = own // targets
    for t in range(sems.shape[0]):
        copies[t].wait()
        total = jnp.zeros((tile, LANES), F32)
        for k in range(slices):
            block = held[k, t * tile : (t + 1) * tile, :]
            hi = block.astype(BF16)
            lo = (block - hi.astype(F32)).astype(BF16)
            w = weights[k]
            total += jnp.dot(hi, w, preferred_element_type=F32)
            total += jnp.dot(lo, w, preferred_element_type=F32)
        total += swap(total)
        for s in range(tile // share):
            upper = total[s * share : s * share + HALF]
            lower = total[s * share + HALF : (s + 1) * share]
            out_ref[t * (tile // share) + s, :HALF, :] = jnp.where(left, upper, lower)

    flat = rows_ref[...].reshape(peers * HALF, LANES)
    both = lax.dot_general(
        flat, flat, (((0,), (0,)), ((), ())),
        precision=lax.Precision.HIGHEST, preferred_element_type=F32,
    )
    outer = lax.dot_general(
        third, third, (((0,), (0,)), ((), ())),
        precision=lax.Precision.HIGHEST, preferred_element_type=F32,
    )
    gram = (both[:RANK, :RANK] + both[RANK:, RANK:]) * outer
    packed = jnp.concatenate([gram[:HALF], gram[HALF:]], axis=1)
    for peer in range(targets):
        out_ref[peer, HALF:, :] = packed


def solve_kernel(got_ref, out_ref):
    total = got_ref[0]
    for peer in range(1, got_ref.shape[0]):
        total = total + got_ref[peer]
    moved = jnp.transpose(jnp.concatenate([total[:HALF]] * 4, axis=0))
    rhs = jnp.concatenate([moved[:RANK, :HALF], moved[RANK:, :HALF]], axis=1)
    gram = jnp.concatenate([total[HALF:, :RANK], total[HALF:, RANK:]], axis=0)
    system = jnp.concatenate([gram, rhs], axis=1)
    strips = RANK // STRIP
    a = [system[STRIP * q : STRIP * (q + 1)] for q in range(strips)]
    row_id = lax.broadcasted_iota(jnp.int32, (STRIP, LANES), 0)
    for p in range(strips):
        cols = [
            [
                jnp.broadcast_to(a[q][:, STRIP * p + m : STRIP * p + m + 1], (STRIP, LANES))
                for m in range(STRIP)
            ]
            for q in range(strips)
        ]
        diag = cols[p]
        piv = a[p]
        for j in range(STRIP):
            inv = 1.0 / jnp.broadcast_to(diag[j][j : j + 1, :], (STRIP, LANES))
            ratio = jnp.where(row_id == j, 1.0 - inv, diag[j] * inv)
            for m in range(j + 1, STRIP):
                diag[m] = diag[m] - ratio * diag[m][j : j + 1, :]
            piv = piv - ratio * piv[j : j + 1, :]
        a[p] = piv
        for q in range(strips):
            if q != p:
                x = a[q]
                for m in range(STRIP):
                    x = x - cols[q][m] * piv[m : m + 1, :]
                a[q] = x
    solved = jnp.concatenate(a, axis=0)
    out_ref[...] = jnp.transpose(jnp.concatenate([solved, solved], axis=0))[RANK:, :RANK]


def body(tensor, second, third):
    rows = lax.axis_size("row")
    cols = lax.axis_size("col")
    slices, own, inner = tensor.shape
    copies = pl.pallas_call(
        pack_kernel,
        out_shape=jax.ShapeDtypeStruct((rows, HALF, LANES), F32),
        in_specs=[vmem()],
        out_specs=vmem(),
    )(second)
    block = lax.all_to_all(copies, "row", 0, 0)
    sent = pl.pallas_call(
        product_kernel,
        out_shape=jax.ShapeDtypeStruct((cols, 2 * HALF, LANES), F32),
        in_specs=[pl.BlockSpec(memory_space=pl.ANY), vmem(), vmem()],
        out_specs=vmem(),
        scratch_shapes=[
            pltpu.VMEM((slices, own, inner), F32),
            pltpu.VMEM((slices, inner, LANES), BF16),
            pltpu.SemaphoreType.DMA((4,)),
        ],
        compiler_params=pltpu.CompilerParams(vmem_limit_bytes=40 << 20),
    )(tensor, block, third)
    got = lax.all_to_all(sent, "col", 0, 0)
    return pl.pallas_call(
        solve_kernel,
        out_shape=jax.ShapeDtypeStruct((RANK, RANK), F32),
        in_specs=[vmem()],
        out_specs=vmem(),
    )(got)


def solution(mesh):
    in_specs = (P(None, "row", "col"), P(("col", "row"), None), P())
    out_specs = P(("row", "col"), None)
    return jax.shard_map(body, mesh=mesh, in_specs=in_specs, out_specs=out_specs, check_vma=False)
```

```python
import jax
import jax.numpy as jnp
from jax import lax
from jax.experimental import pallas as pl
from jax.experimental.pallas import tpu as pltpu
from jax.sharding import PartitionSpec as P

F32 = jnp.float32
BF16 = jnp.bfloat16
RANK = 64
LANES = 128
HALF = 32
STRIP = 8
GROUP = 4


def vmem():
    return pl.BlockSpec(memory_space=pltpu.VMEM)


def limit(mib):
    return pltpu.CompilerParams(vmem_limit_bytes=mib << 20)


def pack_kernel(second_ref, third_ref, out_ref, scale_ref):
    packed = jnp.concatenate([second_ref[:HALF, :], second_ref[HALF:, :]], axis=1)
    for peer in range(out_ref.shape[0]):
        out_ref[peer] = packed
    slices = third_ref.shape[0]
    scale_ref[:slices, :RANK] = third_ref[...]
    scale_ref[:slices, RANK:] = third_ref[...]


def swap(x):
    return pltpu.roll(x, RANK, 1)


def lower_lanes(rows):
    return lax.broadcasted_iota(jnp.int32, (rows, LANES), 1) < RANK


def make_weights(rows_ref, scale_ref, weights):
    left = lower_lanes(HALF)
    for peer in range(rows_ref.shape[0]):
        here = rows_ref[peer]
        there = swap(here)
        for k in range(weights.shape[0]):
            a = here * scale_ref[k : k + 1, :]
            b = there * scale_ref[k : k + 1, :]
            a_hi = a.astype(BF16).astype(F32)
            b_hi = b.astype(BF16).astype(F32)
            first = jnp.where(left, a_hi, b - b_hi)
            other = jnp.where(left, b_hi, a - a_hi)
            base = peer * RANK
            weights[k, base : base + HALF, :] = first.astype(BF16)
            weights[k, base + HALF : base + RANK, :] = other.astype(BF16)


def multiply(held, weights, out_ref, group):
    left = lower_lanes(HALF)
    total = jnp.zeros((GROUP * RANK, LANES), F32)
    for k in range(weights.shape[0]):
        block = held[k, group * GROUP * RANK : (group + 1) * GROUP * RANK, :]
        high = block.astype(BF16)
        low = (block - high.astype(F32)).astype(BF16)
        w = weights[k]
        total += jnp.dot(high, w, preferred_element_type=F32)
        total += jnp.dot(low, w, preferred_element_type=F32)
    total += swap(total)
    for s in range(GROUP):
        upper = total[s * RANK : s * RANK + HALF]
        lower = total[s * RANK + HALF : (s + 1) * RANK]
        out_ref[group * GROUP + s] = jnp.where(left, upper, lower)


def partner_kernel(tensor_ref, rows_ref, scale_ref, out_ref, weights, held, other, sems):
    chips = out_ref.shape[0] - 1
    core = lax.rem(lax.axis_index("col"), 2)
    copies = []
    for turn, (buffer, side) in enumerate(((other, 1 - core), (held, core))):
        for chip in range(chips):
            start = pl.multiple_of(chip * 2 * RANK + side * RANK, RANK)
            copy = pltpu.make_async_copy(
                tensor_ref.at[:, pl.ds(start, RANK)],
                buffer.at[:, pl.ds(chip * RANK, RANK)],
                sems.at[turn * chips + chip],
            )
            copy.start()
            copies.append(copy)
    make_weights(rows_ref, scale_ref, weights)

    flat = rows_ref[...].reshape(-1, LANES)
    both = lax.dot_general(
        flat, flat, (((0,), (0,)), ((), ())),
        precision=lax.Precision.HIGHEST, preferred_element_type=F32,
    )
    third = scale_ref[: weights.shape[0], :]
    outer = lax.dot_general(
        third, third, (((0,), (0,)), ((), ())),
        precision=lax.Precision.HIGHEST, preferred_element_type=F32,
    )
    gram = (both[:RANK, :RANK] + both[RANK:, RANK:]) * outer[:RANK, :RANK]
    out_ref[chips] = jnp.concatenate([gram[:HALF], gram[HALF:]], axis=1)

    for group in range(chips // GROUP):
        for s in range(GROUP):
            copies[group * GROUP + s].wait()
        multiply(other, weights, out_ref, group)
    for chip in range(chips):
        copies[chips + chip].wait()


def own_kernel(held, weights, out_ref):
    for group in range(out_ref.shape[0] // GROUP):
        multiply(held, weights, out_ref, group)


def join_kernel(own_ref, theirs_ref, got_ref, out_ref):
    chips = own_ref.shape[0]
    gram = theirs_ref[chips] + got_ref[chips]
    for chip in range(chips):
        out_ref[chip, :HALF, :] = own_ref[chip] + got_ref[chip]
        out_ref[chip, HALF:, :] = gram


def solve_kernel(got_ref, out_ref):
    total = got_ref[0]
    for peer in range(1, got_ref.shape[0]):
        total = total + got_ref[peer]
    moved = jnp.transpose(jnp.concatenate([total[:HALF]] * 4, axis=0))
    rhs = jnp.concatenate([moved[:RANK, :HALF], moved[RANK:, :HALF]], axis=1)
    gram = jnp.concatenate([total[HALF:, :RANK], total[HALF:, RANK:]], axis=0)
    system = jnp.concatenate([gram, rhs], axis=1)
    strips = RANK // STRIP
    a = [system[STRIP * q : STRIP * (q + 1)] for q in range(strips)]
    row_id = lax.broadcasted_iota(jnp.int32, (STRIP, LANES), 0)
    for p in range(strips):
        cols = [
            [
                jnp.broadcast_to(a[q][:, STRIP * p + m : STRIP * p + m + 1], (STRIP, LANES))
                for m in range(STRIP)
            ]
            for q in range(strips)
        ]
        diag = cols[p]
        piv = a[p]
        for j in range(STRIP):
            inv = 1.0 / jnp.broadcast_to(diag[j][j : j + 1, :], (STRIP, LANES))
            ratio = jnp.where(row_id == j, 1.0 - inv, diag[j] * inv)
            for m in range(j + 1, STRIP):
                diag[m] = diag[m] - ratio * diag[m][j : j + 1, :]
            piv = piv - ratio * piv[j : j + 1, :]
        a[p] = piv
        for q in range(strips):
            if q != p:
                x = a[q]
                for m in range(STRIP):
                    x = x - cols[q][m] * piv[m : m + 1, :]
                a[q] = x
    solved = jnp.concatenate(a, axis=0)
    out_ref[...] = jnp.transpose(jnp.concatenate([solved, solved], axis=0))[RANK:, :RANK]


def shape(*dims, dtype=F32):
    return jax.ShapeDtypeStruct(dims, dtype)


def body(tensor, second, third):
    rows = lax.axis_size("row")
    cols = lax.axis_size("col")
    chips = cols // 2
    slices, own, inner = tensor.shape
    copies, scale = pl.pallas_call(
        pack_kernel,
        out_shape=(shape(rows, HALF, LANES), shape(STRIP, LANES)),
        in_specs=[vmem(), vmem()],
        out_specs=(vmem(), vmem()),
        compiler_params=limit(4),
    )(second, third)
    block = lax.all_to_all(copies, "row", 0, 0)
    theirs, weights, held = pl.pallas_call(
        partner_kernel,
        out_shape=(
            shape(chips + 1, HALF, LANES),
            shape(slices, inner, LANES, dtype=BF16),
            shape(slices, own // 2, inner),
        ),
        in_specs=[pl.BlockSpec(memory_space=pl.ANY), vmem(), vmem()],
        out_specs=(vmem(), vmem(), vmem()),
        scratch_shapes=[
            pltpu.VMEM((slices, own // 2, inner), F32),
            pltpu.SemaphoreType.DMA((cols,)),
        ],
        compiler_params=limit(16),
        cost_estimate=pl.CostEstimate(flops=0, bytes_accessed=8 << 20, transcendentals=0),
    )(pltpu.with_memory_space_constraint(tensor, pltpu.HBM), block, scale)
    got = lax.ppermute(theirs, "col", [(i, i ^ 1) for i in range(cols)])
    mine = pl.pallas_call(
        own_kernel,
        out_shape=shape(chips, HALF, LANES),
        in_specs=[vmem(), vmem()],
        out_specs=vmem(),
        compiler_params=limit(8),
        cost_estimate=pl.CostEstimate(flops=0, bytes_accessed=8 << 20, transcendentals=0),
    )(held, weights)
    sent = pl.pallas_call(
        join_kernel,
        out_shape=shape(chips, 2 * HALF, LANES),
        in_specs=[vmem(), vmem(), vmem()],
        out_specs=vmem(),
        compiler_params=limit(4),
    )(mine, theirs, got)
    sides = [[2 * chip + core for chip in range(chips)] for core in range(2)]
    total = lax.all_to_all(sent, "col", 0, 0, axis_index_groups=sides)
    return pl.pallas_call(
        solve_kernel,
        out_shape=shape(RANK, RANK),
        in_specs=[vmem()],
        out_specs=vmem(),
        compiler_params=limit(4),
    )(total)


def solution(mesh):
    in_specs = (P(None, "row", "col"), P(("col", "row"), None), P())
    out_specs = P(("row", "col"), None)
    return jax.shard_map(body, mesh=mesh, in_specs=in_specs, out_specs=out_specs, check_vma=False)
```

```python
import jax
import jax.numpy as jnp
from jax import lax
from jax.experimental import pallas as pl
from jax.experimental.pallas import tpu as pltpu
from jax.sharding import PartitionSpec as P

F32 = jnp.float32
BF16 = jnp.bfloat16
RANK = 64
LANES = 128
HALF = 32
STRIP = 8
GROUP = 4
GRAM_ROWS = 24


def vmem():
    return pl.BlockSpec(memory_space=pltpu.VMEM)


def anywhere():
    return pl.BlockSpec(memory_space=pl.ANY)


def in_hbm(x):
    return pltpu.with_memory_space_constraint(x, pltpu.HBM)


def limit(mib):
    return pltpu.CompilerParams(vmem_limit_bytes=mib << 20)


def shape(*dims, dtype=F32):
    return jax.ShapeDtypeStruct(dims, dtype)


def pack_kernel(second_ref, out_ref):
    packed = jnp.concatenate([second_ref[:HALF, :], second_ref[HALF:, :]], axis=1)
    for peer in range(out_ref.shape[0]):
        out_ref[peer] = packed


def swap(x):
    return pltpu.roll(x, RANK, 1)


def lower_lanes(rows):
    return lax.broadcasted_iota(jnp.int32, (rows, LANES), 1) < RANK


def make_weights(rows_ref, scale, weights):
    left = lower_lanes(HALF)
    for peer in range(rows_ref.shape[0]):
        here = rows_ref[peer]
        there = swap(here)
        for k in range(weights.shape[0]):
            a = here * scale[k : k + 1, :]
            b = there * scale[k : k + 1, :]
            a_hi = a.astype(BF16).astype(F32)
            b_hi = b.astype(BF16).astype(F32)
            first = jnp.where(left, a_hi, b - b_hi)
            other = jnp.where(left, b_hi, a - a_hi)
            base = peer * RANK
            weights[k, base : base + HALF, :] = first.astype(BF16)
            weights[k, base + HALF : base + RANK, :] = other.astype(BF16)


def multiply(tensor_ref, weights, out_ref, first, side):
    left = lower_lanes(HALF)
    total = jnp.zeros((GROUP * RANK, LANES), F32)
    for k in range(weights.shape[0]):
        block = jnp.concatenate(
            [
                tensor_ref[k, pl.ds(pl.multiple_of((2 * chip + side) * RANK, RANK), RANK), :]
                for chip in range(first, first + GROUP)
            ],
            axis=0,
        )
        high = block.astype(BF16)
        low = (block - high.astype(F32)).astype(BF16)
        w = weights[k]
        total += jnp.dot(high, w, preferred_element_type=F32)
        total += jnp.dot(low, w, preferred_element_type=F32)
    total += swap(total)
    for s in range(GROUP):
        upper = total[s * RANK : s * RANK + HALF]
        lower = total[s * RANK + HALF : (s + 1) * RANK]
        out_ref[(first + s) * HALF : (first + s + 1) * HALF, :] = jnp.where(left, upper, lower)


def pack_gram(gram):
    quarter = HALF // 4
    top = jnp.concatenate([gram[: HALF // 2], gram[HALF // 2 : HALF]], axis=1)
    corner = [
        gram[HALF + quarter * b : HALF + quarter * (b + 1), HALF:] for b in range(4)
    ]
    return jnp.concatenate([top, jnp.concatenate(corner, axis=1)], axis=0)


def partner_kernel(tensor_ref, rows_ref, third_ref, out_ref, weights, scale, sem):
    core = lax.rem(lax.axis_index("col"), 2)
    slices = weights.shape[0]
    copy = pltpu.make_async_copy(third_ref, scale.at[:slices, :], sem)
    copy.start()
    flat = rows_ref[...].reshape(-1, LANES)
    both = lax.dot_general(
        flat, flat, (((0,), (0,)), ((), ())),
        precision=lax.Precision.HIGHEST, preferred_element_type=F32,
    )
    copy.wait()
    third = scale[:slices, :]
    outer = lax.dot_general(
        third, third, (((0,), (0,)), ((), ())),
        precision=lax.Precision.HIGHEST, preferred_element_type=F32,
    )
    gram = (both[:RANK, :RANK] + both[RANK:, RANK:]) * outer
    out_ref[2 * GROUP * HALF :, :] = pack_gram(gram)
    make_weights(rows_ref, jnp.concatenate([third, third], axis=1), weights)
    for first in range(0, 2 * GROUP, GROUP):
        multiply(tensor_ref, weights, out_ref, first, 1 - core)


def own_kernel(tensor_ref, weights, out_ref):
    core = lax.rem(lax.axis_index("col"), 2)
    for first in range(0, 2 * GROUP, GROUP):
        multiply(tensor_ref, weights, out_ref, first, core)


def join_kernel(own_ref, theirs_ref, got_ref, out_ref):
    chips = out_ref.shape[0]
    gram = theirs_ref[chips * HALF :, :] + got_ref[chips * HALF :, :]
    for chip in range(chips):
        part = slice(chip * HALF, (chip + 1) * HALF)
        out_ref[chip, :HALF, :] = own_ref[part, :] + got_ref[part, :]
        out_ref[chip, HALF:, :] = gram


def lane(x, c):
    return jnp.broadcast_to(x[:, c : c + 1], (STRIP, LANES))


def pairwise(terms):
    while len(terms) > 1:
        terms = [terms[i] + terms[i + 1] for i in range(0, len(terms), 2)]
    return terms[0]


def eliminate(diag, others, row_id):
    diag = list(diag)
    for j in range(STRIP):
        inv = 1.0 / jnp.broadcast_to(diag[j][j : j + 1, :], (STRIP, LANES))
        ratio = jnp.where(row_id == j, 1.0 - inv, diag[j] * inv)
        for m in range(j + 1, STRIP):
            diag[m] = diag[m] - ratio * diag[m][j : j + 1, :]
        others = [x - ratio * x[j : j + 1, :] for x in others]
    return others


def solve_kernel(got_ref, out_ref):
    total = pairwise([got_ref[peer] for peer in range(got_ref.shape[0])])
    moved = jnp.transpose(jnp.concatenate([total[:HALF]] * 4, axis=0))
    rhs = jnp.concatenate([moved[:RANK, :HALF], moved[RANK:, :HALF]], axis=1)
    top = total[HALF : HALF + HALF // 2]
    corner = total[HALF + HALF // 2 :]
    upper = jnp.concatenate([top[:, :RANK], top[:, RANK:]], axis=0)
    beside = jnp.transpose(upper[:, HALF:])
    below = jnp.concatenate([corner[:, HALF * b : HALF * (b + 1)] for b in range(4)], axis=0)
    lower = jnp.concatenate([beside, below], axis=1)
    system = jnp.concatenate([jnp.concatenate([upper, lower], axis=0), rhs], axis=1)
    strips = RANK // STRIP
    a = [system[STRIP * q : STRIP * (q + 1)] for q in range(strips)]
    row_id = lax.broadcasted_iota(jnp.int32, (STRIP, LANES), 0)
    diag = [lane(a[0], m) for m in range(STRIP)]
    for p in range(strips):
        base = STRIP * p
        cols = [
            [lane(a[q], base + m) for m in range(STRIP)] if q != p else None
            for q in range(strips)
        ]
        ahead = []
        if p + 1 < strips:
            ahead = [lane(a[p], base + STRIP + m) for m in range(STRIP)]
            old = [lane(a[p + 1], base + STRIP + m) for m in range(STRIP)]
        pivot, *ahead = eliminate(diag, [a[p]] + ahead, row_id)
        a[p] = pivot
        if p + 1 < strips:
            diag = [
                old[m]
                - pairwise([cols[p + 1][k] * ahead[m][k : k + 1, :] for k in range(STRIP)])
                for m in range(STRIP)
            ]
        for q in range(strips):
            if q != p:
                a[q] = a[q] - pairwise(
                    [cols[q][m] * pivot[m : m + 1, :] for m in range(STRIP)]
                )
    solved = jnp.concatenate(a, axis=0)
    out_ref[...] = jnp.transpose(jnp.concatenate([solved, solved], axis=0))[RANK:, :RANK]


def body(tensor, second, third):
    rows = lax.axis_size("row")
    cols = lax.axis_size("col")
    chips = cols // 2
    slices, own, inner = tensor.shape
    pairs = [(i, i ^ 1) for i in range(cols)]
    second, tensor = lax.optimization_barrier((lax.ppermute(second, "col", pairs), tensor))
    tensor = lax.ppermute(tensor, "col", pairs)
    copies = pl.pallas_call(
        pack_kernel,
        out_shape=shape(rows, HALF, LANES),
        in_specs=[vmem()],
        out_specs=vmem(),
        compiler_params=limit(4),
    )(second)
    block = lax.all_to_all(copies, "row", 0, 0)
    theirs, weights = pl.pallas_call(
        partner_kernel,
        out_shape=(
            shape(chips * HALF + GRAM_ROWS, LANES),
            shape(slices, inner, LANES, dtype=BF16),
        ),
        in_specs=[vmem(), vmem(), anywhere()],
        out_specs=(vmem(), vmem()),
        scratch_shapes=[pltpu.VMEM((STRIP, RANK), F32), pltpu.SemaphoreType.DMA],
        compiler_params=limit(12),
        cost_estimate=pl.CostEstimate(flops=0, bytes_accessed=4 << 20, transcendentals=0),
    )(tensor, block, in_hbm(third))
    got = lax.ppermute(theirs, "col", pairs)
    mine = pl.pallas_call(
        own_kernel,
        out_shape=shape(chips * HALF, LANES),
        in_specs=[vmem(), vmem()],
        out_specs=vmem(),
        compiler_params=limit(12),
        cost_estimate=pl.CostEstimate(flops=0, bytes_accessed=4 << 20, transcendentals=0),
    )(tensor, weights)
    sent = pl.pallas_call(
        join_kernel,
        out_shape=shape(chips, HALF + GRAM_ROWS, LANES),
        in_specs=[vmem(), vmem(), vmem()],
        out_specs=vmem(),
        compiler_params=limit(4),
    )(mine, theirs, got)
    sides = [[2 * chip + core for chip in range(chips)] for core in range(2)]
    total = lax.all_to_all(sent, "col", 0, 0, axis_index_groups=sides)
    return pl.pallas_call(
        solve_kernel,
        out_shape=shape(RANK, RANK),
        in_specs=[vmem()],
        out_specs=vmem(),
        compiler_params=limit(4),
    )(total)


def solution(mesh):
    in_specs = (P(None, "row", "col"), P(("col", "row"), None), P())
    out_specs = P(("row", "col"), None)
    return jax.shard_map(body, mesh=mesh, in_specs=in_specs, out_specs=out_specs, check_vma=False)
```

```python
import jax
import jax.numpy as jnp
from jax import lax
from jax.experimental import pallas as pl
from jax.experimental.pallas import tpu as pltpu
from jax.sharding import PartitionSpec as P

F32 = jnp.float32
BF16 = jnp.bfloat16
RANK = 64
LANES = 128
HALF = 32
STRIP = 8
GROUP = 4
GRAM_ROWS = 24
CHIPS = (5, 6, 7, 0, 1, 2, 3, 4)
PLANE = (10, 11, 12, 13, 14, 15, 0, 1, 2, 3, 4, 5, 6, 7, 8, 9)


def vmem():
    return pl.BlockSpec(memory_space=pltpu.VMEM)


def anywhere():
    return pl.BlockSpec(memory_space=pl.ANY)


def in_hbm(x):
    return pltpu.with_memory_space_constraint(x, pltpu.HBM)


def limit(mib):
    return pltpu.CompilerParams(vmem_limit_bytes=mib << 20)


def shape(*dims, dtype=F32):
    return jax.ShapeDtypeStruct(dims, dtype)


def scale_kernel(third_ref, out_ref):
    slices = third_ref.shape[0]
    out_ref[:slices, :RANK] = third_ref[...]
    out_ref[:slices, RANK:] = third_ref[...]


def pack_kernel(second_ref, scale_ref, out_ref):
    del scale_ref
    packed = jnp.concatenate([second_ref[:HALF, :], second_ref[HALF:, :]], axis=1)
    for peer in range(out_ref.shape[0]):
        out_ref[peer] = packed


def swap(x):
    return pltpu.roll(x, RANK, 1)


def lower_lanes(rows):
    return lax.broadcasted_iota(jnp.int32, (rows, LANES), 1) < RANK


def make_weights(rows_ref, scale_ref, weights):
    left = lower_lanes(HALF)
    for slot, peer in enumerate(PLANE):
        here = rows_ref[slot]
        there = swap(here)
        for k in range(weights.shape[0]):
            a = here * scale_ref[k : k + 1, :]
            b = there * scale_ref[k : k + 1, :]
            a_hi = a.astype(BF16).astype(F32)
            b_hi = b.astype(BF16).astype(F32)
            first = jnp.where(left, a_hi, b - b_hi)
            other = jnp.where(left, b_hi, a - a_hi)
            base = peer * RANK
            weights[k, base : base + HALF, :] = first.astype(BF16)
            weights[k, base + HALF : base + RANK, :] = other.astype(BF16)


def multiply(tensor_ref, weights, out_ref, first, side):
    left = lower_lanes(HALF)
    total = jnp.zeros((GROUP * RANK, LANES), F32)
    for k in range(weights.shape[0]):
        block = jnp.concatenate(
            [
                tensor_ref[k, pl.ds(pl.multiple_of((2 * chip + side) * RANK, RANK), RANK), :]
                for chip in range(first, first + GROUP)
            ],
            axis=0,
        )
        high = block.astype(BF16)
        low = (block - high.astype(F32)).astype(BF16)
        w = weights[k]
        total += jnp.dot(high, w, preferred_element_type=F32)
        total += jnp.dot(low, w, preferred_element_type=F32)
    total += swap(total)
    for s in range(GROUP):
        upper = total[s * RANK : s * RANK + HALF]
        lower = total[s * RANK + HALF : (s + 1) * RANK]
        out_ref[(first + s) * HALF : (first + s + 1) * HALF, :] = jnp.where(left, upper, lower)


def pack_gram(gram):
    quarter = HALF // 4
    top = jnp.concatenate([gram[: HALF // 2], gram[HALF // 2 : HALF]], axis=1)
    corner = [
        gram[HALF + quarter * b : HALF + quarter * (b + 1), HALF:] for b in range(4)
    ]
    return jnp.concatenate([top, jnp.concatenate(corner, axis=1)], axis=0)


def partner_kernel(tensor_ref, rows_ref, scale_ref, out_ref, weights):
    core = lax.rem(lax.axis_index("col"), 2)
    make_weights(rows_ref, scale_ref, weights)
    flat = rows_ref[...].reshape(-1, LANES)
    both = lax.dot_general(
        flat, flat, (((0,), (0,)), ((), ())),
        precision=lax.Precision.HIGHEST, preferred_element_type=F32,
    )
    third = scale_ref[: weights.shape[0], :]
    outer = lax.dot_general(
        third, third, (((0,), (0,)), ((), ())),
        precision=lax.Precision.HIGHEST, preferred_element_type=F32,
    )
    gram = (both[:RANK, :RANK] + both[RANK:, RANK:]) * outer[:RANK, :RANK]
    out_ref[2 * GROUP * HALF :, :] = pack_gram(gram)
    for first in range(0, 2 * GROUP, GROUP):
        multiply(tensor_ref, weights, out_ref, first, 1 - core)


def own_kernel(tensor_ref, weights, out_ref):
    core = lax.rem(lax.axis_index("col"), 2)
    for first in range(0, 2 * GROUP, GROUP):
        multiply(tensor_ref, weights, out_ref, first, core)


def join_kernel(own_ref, theirs_ref, got_ref, out_ref):
    chips = out_ref.shape[0]
    gram = theirs_ref[chips * HALF :, :] + got_ref[chips * HALF :, :]
    for chip in range(chips):
        part = slice(chip * HALF, (chip + 1) * HALF)
        slot = CHIPS.index(chip)
        out_ref[slot, :HALF, :] = own_ref[part, :] + got_ref[part, :]
        out_ref[slot, HALF:, :] = gram


def lane(x, c):
    return jnp.broadcast_to(x[:, c : c + 1], (STRIP, LANES))


def pairwise(terms):
    while len(terms) > 1:
        terms = [terms[i] + terms[i + 1] for i in range(0, len(terms), 2)]
    return terms[0]


def eliminate(diag, others, row_id):
    diag = list(diag)
    for j in range(STRIP):
        inv = 1.0 / jnp.broadcast_to(diag[j][j : j + 1, :], (STRIP, LANES))
        ratio = jnp.where(row_id == j, 1.0 - inv, diag[j] * inv)
        for m in range(j + 1, STRIP):
            diag[m] = diag[m] - ratio * diag[m][j : j + 1, :]
        others = [x - ratio * x[j : j + 1, :] for x in others]
    return others


def solve_kernel(got_ref, out_ref):
    total = pairwise([got_ref[peer] for peer in range(got_ref.shape[0])])
    moved = jnp.transpose(jnp.concatenate([total[:HALF]] * 4, axis=0))
    rhs = jnp.concatenate([moved[:RANK, :HALF], moved[RANK:, :HALF]], axis=1)
    top = total[HALF : HALF + HALF // 2]
    corner = total[HALF + HALF // 2 :]
    upper = jnp.concatenate([top[:, :RANK], top[:, RANK:]], axis=0)
    beside = jnp.transpose(upper[:, HALF:])
    below = jnp.concatenate([corner[:, HALF * b : HALF * (b + 1)] for b in range(4)], axis=0)
    lower = jnp.concatenate([beside, below], axis=1)
    system = jnp.concatenate([jnp.concatenate([upper, lower], axis=0), rhs], axis=1)
    strips = RANK // STRIP
    a = [system[STRIP * q : STRIP * (q + 1)] for q in range(strips)]
    row_id = lax.broadcasted_iota(jnp.int32, (STRIP, LANES), 0)
    diag = [lane(a[0], m) for m in range(STRIP)]
    for p in range(strips):
        base = STRIP * p
        cols = [
            [lane(a[q], base + m) for m in range(STRIP)] if q != p else None
            for q in range(strips)
        ]
        ahead = []
        if p + 1 < strips:
            ahead = [lane(a[p], base + STRIP + m) for m in range(STRIP)]
            old = [lane(a[p + 1], base + STRIP + m) for m in range(STRIP)]
        pivot, *ahead = eliminate(diag, [a[p]] + ahead, row_id)
        a[p] = pivot
        if p + 1 < strips:
            diag = [
                old[m]
                - pairwise([cols[p + 1][k] * ahead[m][k : k + 1, :] for k in range(STRIP)])
                for m in range(STRIP)
            ]
        for q in range(strips):
            if q != p:
                a[q] = a[q] - pairwise(
                    [cols[q][m] * pivot[m : m + 1, :] for m in range(STRIP)]
                )
    solved = jnp.concatenate(a, axis=0)
    out_ref[...] = jnp.transpose(jnp.concatenate([solved, solved], axis=0))[RANK:, :RANK]


def body(tensor, second, third):
    rows = lax.axis_size("row")
    cols = lax.axis_size("col")
    chips = cols // 2
    slices, own, inner = tensor.shape
    pairs = [(i, i ^ 1) for i in range(cols)]
    second = lax.ppermute(second, "col", pairs)
    scale = pl.pallas_call(
        scale_kernel,
        out_shape=shape(STRIP, LANES),
        in_specs=[vmem()],
        out_specs=vmem(),
        compiler_params=limit(4),
        cost_estimate=pl.CostEstimate(flops=0, bytes_accessed=4 << 20, transcendentals=0),
    )(third)
    second, scale, tensor = lax.optimization_barrier((second, scale, tensor))
    tensor = lax.ppermute(tensor, "col", pairs)
    copies = pl.pallas_call(
        pack_kernel,
        out_shape=shape(rows, HALF, LANES),
        in_specs=[vmem(), vmem()],
        out_specs=vmem(),
        compiler_params=limit(4),
    )(second, scale)
    block = lax.all_to_all(copies, "row", 0, 0, axis_index_groups=[list(PLANE)])
    theirs, weights = pl.pallas_call(
        partner_kernel,
        out_shape=(
            shape(chips * HALF + GRAM_ROWS, LANES),
            shape(slices, inner, LANES, dtype=BF16),
        ),
        in_specs=[vmem(), vmem(), vmem()],
        out_specs=(vmem(), vmem()),
        compiler_params=limit(12),
        cost_estimate=pl.CostEstimate(flops=0, bytes_accessed=4 << 20, transcendentals=0),
    )(tensor, block, scale)
    got = lax.ppermute(theirs, "col", pairs)
    mine = pl.pallas_call(
        own_kernel,
        out_shape=shape(chips * HALF, LANES),
        in_specs=[vmem(), vmem()],
        out_specs=vmem(),
        compiler_params=limit(12),
        cost_estimate=pl.CostEstimate(flops=0, bytes_accessed=4 << 20, transcendentals=0),
    )(tensor, weights)
    sent = pl.pallas_call(
        join_kernel,
        out_shape=shape(chips, HALF + GRAM_ROWS, LANES),
        in_specs=[vmem(), vmem(), vmem()],
        out_specs=vmem(),
        compiler_params=limit(4),
    )(mine, theirs, got)
    sides = [[2 * chip + core for chip in CHIPS] for core in range(2)]
    total = lax.all_to_all(sent, "col", 0, 0, axis_index_groups=sides)
    return pl.pallas_call(
        solve_kernel,
        out_shape=shape(RANK, RANK),
        in_specs=[vmem()],
        out_specs=vmem(),
        compiler_params=limit(4),
    )(total)


def solution(mesh):
    in_specs = (P(None, "row", "col"), P(("col", "row"), None), P())
    out_specs = P(("row", "col"), None)
    return jax.shard_map(body, mesh=mesh, in_specs=in_specs, out_specs=out_specs, check_vma=False)
```

```python
import jax
import jax.numpy as jnp
from jax import lax
from jax.experimental import pallas as pl
from jax.experimental.pallas import tpu as pltpu
from jax.sharding import PartitionSpec as P

F32 = jnp.float32
BF16 = jnp.bfloat16
RANK = 64
LANES = 128
HALF = 32
STRIP = 8
GROUP = 4
GRAM_ROWS = 24
CHIPS = (5, 6, 4, 7, 0, 3, 1, 2)
PLANE = (10, 11, 12, 13, 14, 15, 0, 1, 2, 3, 4, 5, 6, 7, 8, 9)


def vmem():
    return pl.BlockSpec(memory_space=pltpu.VMEM)


def anywhere():
    return pl.BlockSpec(memory_space=pl.ANY)


def in_hbm(x):
    return pltpu.with_memory_space_constraint(x, pltpu.HBM)


def limit(mib):
    return pltpu.CompilerParams(vmem_limit_bytes=mib << 20)


def shape(*dims, dtype=F32):
    return jax.ShapeDtypeStruct(dims, dtype)


def scale_kernel(third_ref, out_ref):
    slices = third_ref.shape[0]
    out_ref[:slices, :RANK] = third_ref[...]
    out_ref[:slices, RANK:] = third_ref[...]


def pack_kernel(second_ref, scale_ref, out_ref):
    del scale_ref
    packed = jnp.concatenate([second_ref[:HALF, :], second_ref[HALF:, :]], axis=1)
    for peer in range(out_ref.shape[0]):
        out_ref[peer] = packed


def swap(x):
    return pltpu.roll(x, RANK, 1)


def lower_lanes(rows):
    return lax.broadcasted_iota(jnp.int32, (rows, LANES), 1) < RANK


def make_weights(rows_ref, scale_ref, weights):
    left = lower_lanes(HALF)
    for slot, peer in enumerate(PLANE):
        here = rows_ref[slot]
        there = swap(here)
        for k in range(weights.shape[0]):
            a = here * scale_ref[k : k + 1, :]
            b = there * scale_ref[k : k + 1, :]
            a_hi = a.astype(BF16).astype(F32)
            b_hi = b.astype(BF16).astype(F32)
            first = jnp.where(left, a_hi, b - b_hi)
            other = jnp.where(left, b_hi, a - a_hi)
            base = peer * RANK
            weights[k, base : base + HALF, :] = first.astype(BF16)
            weights[k, base + HALF : base + RANK, :] = other.astype(BF16)


def multiply(tensor_ref, weights, out_ref, first, side):
    left = lower_lanes(HALF)
    total = jnp.zeros((GROUP * RANK, LANES), F32)
    for k in range(weights.shape[0]):
        block = jnp.concatenate(
            [
                tensor_ref[k, pl.ds(pl.multiple_of((2 * chip + side) * RANK, RANK), RANK), :]
                for chip in range(first, first + GROUP)
            ],
            axis=0,
        )
        high = block.astype(BF16)
        low = (block - high.astype(F32)).astype(BF16)
        w = weights[k]
        total += jnp.dot(high, w, preferred_element_type=F32)
        total += jnp.dot(low, w, preferred_element_type=F32)
    total += swap(total)
    for s in range(GROUP):
        upper = total[s * RANK : s * RANK + HALF]
        lower = total[s * RANK + HALF : (s + 1) * RANK]
        out_ref[(first + s) * HALF : (first + s + 1) * HALF, :] = jnp.where(left, upper, lower)


def pack_gram(gram):
    quarter = HALF // 4
    top = jnp.concatenate([gram[: HALF // 2], gram[HALF // 2 : HALF]], axis=1)
    corner = [
        gram[HALF + quarter * b : HALF + quarter * (b + 1), HALF:] for b in range(4)
    ]
    return jnp.concatenate([top, jnp.concatenate(corner, axis=1)], axis=0)


def weights_kernel(rows_ref, scale_ref, weights, gram_ref):
    make_weights(rows_ref, scale_ref, weights)
    flat = rows_ref[...].reshape(-1, LANES)
    both = lax.dot_general(
        flat, flat, (((0,), (0,)), ((), ())),
        precision=lax.Precision.HIGHEST, preferred_element_type=F32,
    )
    third = scale_ref[: weights.shape[0], :]
    outer = lax.dot_general(
        third, third, (((0,), (0,)), ((), ())),
        precision=lax.Precision.HIGHEST, preferred_element_type=F32,
    )
    gram = (both[:RANK, :RANK] + both[RANK:, RANK:]) * outer[:RANK, :RANK]
    gram_ref[...] = pack_gram(gram)


def partner_kernel(tensor_ref, weights, gram_ref, out_ref):
    core = lax.rem(lax.axis_index("col"), 2)
    for first in range(0, 2 * GROUP, GROUP):
        multiply(tensor_ref, weights, out_ref, first, 1 - core)
    out_ref[2 * GROUP * HALF :, :] = gram_ref[...]


def own_kernel(tensor_ref, weights, out_ref):
    core = lax.rem(lax.axis_index("col"), 2)
    for first in range(0, 2 * GROUP, GROUP):
        multiply(tensor_ref, weights, out_ref, first, core)


def join_kernel(own_ref, theirs_ref, got_ref, out_ref):
    chips = out_ref.shape[0]
    gram = theirs_ref[chips * HALF :, :] + got_ref[chips * HALF :, :]
    for chip in range(chips):
        part = slice(chip * HALF, (chip + 1) * HALF)
        slot = CHIPS.index(chip)
        out_ref[slot, :HALF, :] = own_ref[part, :] + got_ref[part, :]
        out_ref[slot, HALF:, :] = gram


def lane(x, c):
    return jnp.broadcast_to(x[:, c : c + 1], (STRIP, LANES))


def pairwise(terms):
    while len(terms) > 1:
        terms = [terms[i] + terms[i + 1] for i in range(0, len(terms), 2)]
    return terms[0]


def eliminate(diag, others, row_id):
    diag = list(diag)
    for j in range(STRIP):
        inv = 1.0 / jnp.broadcast_to(diag[j][j : j + 1, :], (STRIP, LANES))
        ratio = jnp.where(row_id == j, 1.0 - inv, diag[j] * inv)
        for m in range(j + 1, STRIP):
            diag[m] = diag[m] - ratio * diag[m][j : j + 1, :]
        others = [x - ratio * x[j : j + 1, :] for x in others]
    return others


def solve_kernel(got_ref, out_ref):
    total = pairwise([got_ref[peer] for peer in range(got_ref.shape[0])])
    moved = jnp.transpose(jnp.concatenate([total[:HALF]] * 4, axis=0))
    rhs = jnp.concatenate([moved[:RANK, :HALF], moved[RANK:, :HALF]], axis=1)
    top = total[HALF : HALF + HALF // 2]
    corner = total[HALF + HALF // 2 :]
    upper = jnp.concatenate([top[:, :RANK], top[:, RANK:]], axis=0)
    beside = jnp.transpose(upper[:, HALF:])
    below = jnp.concatenate([corner[:, HALF * b : HALF * (b + 1)] for b in range(4)], axis=0)
    lower = jnp.concatenate([beside, below], axis=1)
    system = jnp.concatenate([jnp.concatenate([upper, lower], axis=0), rhs], axis=1)
    strips = RANK // STRIP
    a = [system[STRIP * q : STRIP * (q + 1)] for q in range(strips)]
    row_id = lax.broadcasted_iota(jnp.int32, (STRIP, LANES), 0)
    diag = [lane(a[0], m) for m in range(STRIP)]
    for p in range(strips):
        base = STRIP * p
        cols = [
            [lane(a[q], base + m) for m in range(STRIP)] if q != p else None
            for q in range(strips)
        ]
        ahead = []
        if p + 1 < strips:
            ahead = [lane(a[p], base + STRIP + m) for m in range(STRIP)]
            old = [lane(a[p + 1], base + STRIP + m) for m in range(STRIP)]
        pivot, *ahead = eliminate(diag, [a[p]] + ahead, row_id)
        a[p] = pivot
        if p + 1 < strips:
            diag = [
                old[m]
                - pairwise([cols[p + 1][k] * ahead[m][k : k + 1, :] for k in range(STRIP)])
                for m in range(STRIP)
            ]
        for q in range(strips):
            if q != p:
                a[q] = a[q] - pairwise(
                    [cols[q][m] * pivot[m : m + 1, :] for m in range(STRIP)]
                )
    solved = jnp.concatenate(a, axis=0)
    out_ref[...] = jnp.transpose(jnp.concatenate([solved, solved], axis=0))[RANK:, :RANK]


def body(tensor, second, third):
    rows = lax.axis_size("row")
    cols = lax.axis_size("col")
    chips = cols // 2
    slices, own, inner = tensor.shape
    pairs = [(i, i ^ 1) for i in range(cols)]
    second = lax.ppermute(second, "col", pairs)
    scale = pl.pallas_call(
        scale_kernel,
        out_shape=shape(STRIP, LANES),
        in_specs=[vmem()],
        out_specs=vmem(),
        compiler_params=limit(4),
        cost_estimate=pl.CostEstimate(flops=0, bytes_accessed=4 << 20, transcendentals=0),
    )(third)
    second, scale, tensor = lax.optimization_barrier((second, scale, tensor))
    tensor = lax.ppermute(tensor, "col", pairs)
    copies = pl.pallas_call(
        pack_kernel,
        out_shape=shape(rows, HALF, LANES),
        in_specs=[vmem(), vmem()],
        out_specs=vmem(),
        compiler_params=limit(4),
    )(second, scale)
    block = lax.all_to_all(copies, "row", 0, 0, axis_index_groups=[list(PLANE)])
    weights, gram = pl.pallas_call(
        weights_kernel,
        out_shape=(shape(slices, inner, LANES, dtype=BF16), shape(GRAM_ROWS, LANES)),
        in_specs=[vmem(), vmem()],
        out_specs=(vmem(), vmem()),
        compiler_params=limit(8),
        cost_estimate=pl.CostEstimate(flops=0, bytes_accessed=4 << 20, transcendentals=0),
    )(block, scale)
    theirs = pl.pallas_call(
        partner_kernel,
        out_shape=shape(chips * HALF + GRAM_ROWS, LANES),
        in_specs=[vmem(), vmem(), vmem()],
        out_specs=vmem(),
        compiler_params=limit(12),
        cost_estimate=pl.CostEstimate(flops=0, bytes_accessed=4 << 20, transcendentals=0),
    )(tensor, weights, gram)
    got = lax.ppermute(theirs, "col", pairs)
    mine = pl.pallas_call(
        own_kernel,
        out_shape=shape(chips * HALF, LANES),
        in_specs=[vmem(), vmem()],
        out_specs=vmem(),
        compiler_params=limit(12),
        cost_estimate=pl.CostEstimate(flops=0, bytes_accessed=4 << 20, transcendentals=0),
    )(tensor, weights)
    sent = pl.pallas_call(
        join_kernel,
        out_shape=shape(chips, HALF + GRAM_ROWS, LANES),
        in_specs=[vmem(), vmem(), vmem()],
        out_specs=vmem(),
        compiler_params=limit(4),
    )(mine, theirs, got)
    sides = [[2 * chip + core for chip in CHIPS] for core in range(2)]
    total = lax.all_to_all(sent, "col", 0, 0, axis_index_groups=sides)
    return pl.pallas_call(
        solve_kernel,
        out_shape=shape(RANK, RANK),
        in_specs=[vmem()],
        out_specs=vmem(),
        compiler_params=limit(4),
    )(total)


def solution(mesh):
    in_specs = (P(None, "row", "col"), P(("col", "row"), None), P())
    out_specs = P(("row", "col"), None)
    return jax.shard_map(body, mesh=mesh, in_specs=in_specs, out_specs=out_specs, check_vma=False)
```

```python
import jax
import jax.numpy as jnp
from jax import lax
from jax.experimental import pallas as pl
from jax.experimental.pallas import tpu as pltpu
from jax.sharding import PartitionSpec as P

F32 = jnp.float32
BF16 = jnp.bfloat16
RANK = 64
LANES = 128
HALF = 32
STRIP = 8
GROUP = 4
GRAM_ROWS = 24
CHIPS = (5, 6, 4, 7, 0, 3, 1, 2)
PLANE = (10, 11, 12, 13, 14, 15, 0, 1, 2, 3, 4, 5, 6, 7, 8, 9)


def vmem():
    return pl.BlockSpec(memory_space=pltpu.VMEM)


def anywhere():
    return pl.BlockSpec(memory_space=pl.ANY)


def in_hbm(x):
    return pltpu.with_memory_space_constraint(x, pltpu.HBM)


def limit(mib):
    return pltpu.CompilerParams(vmem_limit_bytes=mib << 20)


def shape(*dims, dtype=F32):
    return jax.ShapeDtypeStruct(dims, dtype)


def scale_kernel(third_ref, out_ref):
    slices = third_ref.shape[0]
    out_ref[:slices, :RANK] = third_ref[...]
    out_ref[:slices, RANK:] = third_ref[...]


def pack_kernel(second_ref, scale_ref, out_ref):
    del scale_ref
    packed = jnp.concatenate([second_ref[:HALF, :], second_ref[HALF:, :]], axis=1)
    for peer in range(out_ref.shape[0]):
        out_ref[peer] = packed


def swap(x):
    return pltpu.roll(x, RANK, 1)


def lower_lanes(rows):
    return lax.broadcasted_iota(jnp.int32, (rows, LANES), 1) < RANK


def make_weights(rows_ref, scale_ref, weights):
    left = lower_lanes(HALF)
    for slot, peer in enumerate(PLANE):
        here = rows_ref[slot]
        there = swap(here)
        for k in range(weights.shape[0]):
            a = here * scale_ref[k : k + 1, :]
            b = there * scale_ref[k : k + 1, :]
            a_hi = a.astype(BF16).astype(F32)
            b_hi = b.astype(BF16).astype(F32)
            first = jnp.where(left, a_hi, b - b_hi)
            other = jnp.where(left, b_hi, a - a_hi)
            base = peer * RANK
            weights[k, base : base + HALF, :] = first.astype(BF16)
            weights[k, base + HALF : base + RANK, :] = other.astype(BF16)


def multiply(tensor_ref, weights, out_ref, first, side):
    left = lower_lanes(HALF)
    total = jnp.zeros((GROUP * RANK, LANES), F32)
    for k in range(weights.shape[0]):
        block = jnp.concatenate(
            [
                tensor_ref[k, pl.ds(pl.multiple_of((2 * chip + side) * RANK, RANK), RANK), :]
                for chip in range(first, first + GROUP)
            ],
            axis=0,
        )
        high = block.astype(BF16)
        low = (block - high.astype(F32)).astype(BF16)
        w = weights[k]
        total += jnp.dot(high, w, preferred_element_type=F32)
        total += jnp.dot(low, w, preferred_element_type=F32)
    total += swap(total)
    for s in range(GROUP):
        upper = total[s * RANK : s * RANK + HALF]
        lower = total[s * RANK + HALF : (s + 1) * RANK]
        out_ref[(first + s) * HALF : (first + s + 1) * HALF, :] = jnp.where(left, upper, lower)


def pack_gram(gram):
    quarter = HALF // 4
    top = jnp.concatenate([gram[: HALF // 2], gram[HALF // 2 : HALF]], axis=1)
    corner = [
        gram[HALF + quarter * b : HALF + quarter * (b + 1), HALF:] for b in range(4)
    ]
    return jnp.concatenate([top, jnp.concatenate(corner, axis=1)], axis=0)


def weights_kernel(rows_ref, scale_ref, weights, gram_ref):
    make_weights(rows_ref, scale_ref, weights)
    flat = rows_ref[...].reshape(-1, LANES)
    both = lax.dot_general(
        flat, flat, (((0,), (0,)), ((), ())),
        precision=lax.Precision.HIGHEST, preferred_element_type=F32,
    )
    third = scale_ref[: weights.shape[0], :]
    outer = lax.dot_general(
        third, third, (((0,), (0,)), ((), ())),
        precision=lax.Precision.HIGHEST, preferred_element_type=F32,
    )
    gram = (both[:RANK, :RANK] + both[RANK:, RANK:]) * outer[:RANK, :RANK]
    gram_ref[...] = pack_gram(gram)


def partner_kernel(tensor_ref, weights, gram_ref, out_ref):
    core = lax.rem(lax.axis_index("col"), 2)
    for first in range(0, 2 * GROUP, GROUP):
        multiply(tensor_ref, weights, out_ref, first, 1 - core)
    out_ref[2 * GROUP * HALF :, :] = gram_ref[...]


def own_kernel(tensor_ref, weights, out_ref):
    core = lax.rem(lax.axis_index("col"), 2)
    for first in range(0, 2 * GROUP, GROUP):
        multiply(tensor_ref, weights, out_ref, first, core)


def join_kernel(own_ref, theirs_ref, got_ref, out_ref):
    chips = out_ref.shape[0]
    gram = theirs_ref[chips * HALF :, :] + got_ref[chips * HALF :, :]
    for chip in range(chips):
        part = slice(chip * HALF, (chip + 1) * HALF)
        slot = CHIPS.index(chip)
        out_ref[slot, :HALF, :] = own_ref[part, :] + got_ref[part, :]
        out_ref[slot, HALF:, :] = gram


def lane(x, c):
    return jnp.broadcast_to(x[:, c : c + 1], (STRIP, LANES))


def pairwise(terms):
    while len(terms) > 1:
        terms = [terms[i] + terms[i + 1] for i in range(0, len(terms), 2)]
    return terms[0]


def eliminate(diag, others, row_id):
    diag = list(diag)
    for j in range(STRIP):
        inv = 1.0 / jnp.broadcast_to(diag[j][j : j + 1, :], (STRIP, LANES))
        ratio = jnp.where(row_id == j, 1.0 - inv, diag[j] * inv)
        for m in range(j + 1, STRIP):
            diag[m] = diag[m] - ratio * diag[m][j : j + 1, :]
        others = [x - ratio * x[j : j + 1, :] for x in others]
    return others


def solve_kernel(got_ref, out_ref):
    total = pairwise([got_ref[peer] for peer in range(got_ref.shape[0])])
    moved = jnp.transpose(jnp.concatenate([total[:HALF]] * 4, axis=0))
    rhs = jnp.concatenate([moved[:RANK, :HALF], moved[RANK:, :HALF]], axis=1)
    top = total[HALF : HALF + HALF // 2]
    corner = total[HALF + HALF // 2 :]
    upper = jnp.concatenate([top[:, :RANK], top[:, RANK:]], axis=0)
    beside = jnp.transpose(upper[:, HALF:])
    below = jnp.concatenate([corner[:, HALF * b : HALF * (b + 1)] for b in range(4)], axis=0)
    lower = jnp.concatenate([beside, below], axis=1)
    system = jnp.concatenate([jnp.concatenate([upper, lower], axis=0), rhs], axis=1)
    strips = RANK // STRIP
    a = [system[STRIP * q : STRIP * (q + 1)] for q in range(strips)]
    row_id = lax.broadcasted_iota(jnp.int32, (STRIP, LANES), 0)
    diag = [lane(a[0], m) for m in range(STRIP)]
    for p in range(strips):
        base = STRIP * p
        cols = [
            [lane(a[q], base + m) for m in range(STRIP)] if q != p else None
            for q in range(strips)
        ]
        ahead = []
        if p + 1 < strips:
            ahead = [lane(a[p], base + STRIP + m) for m in range(STRIP)]
            old = [lane(a[p + 1], base + STRIP + m) for m in range(STRIP)]
        pivot, *ahead = eliminate(diag, [a[p]] + ahead, row_id)
        a[p] = pivot
        if p + 1 < strips:
            diag = [
                old[m]
                - pairwise([cols[p + 1][k] * ahead[m][k : k + 1, :] for k in range(STRIP)])
                for m in range(STRIP)
            ]
        for q in range(strips):
            if q != p:
                a[q] = a[q] - pairwise(
                    [cols[q][m] * pivot[m : m + 1, :] for m in range(STRIP)]
                )
    solved = jnp.concatenate(a, axis=0)
    out_ref[...] = jnp.transpose(jnp.concatenate([solved, solved], axis=0))[RANK:, :RANK]


def body(tensor, second, third):
    rows = lax.axis_size("row")
    cols = lax.axis_size("col")
    chips = cols // 2
    slices, own, inner = tensor.shape
    pairs = [(i, i ^ 1) for i in range(cols)]
    second = lax.ppermute(second, "col", pairs)
    scale = pl.pallas_call(
        scale_kernel,
        out_shape=shape(STRIP, LANES),
        in_specs=[vmem()],
        out_specs=vmem(),
        compiler_params=limit(4),
        cost_estimate=pl.CostEstimate(flops=0, bytes_accessed=4 << 20, transcendentals=0),
    )(third)
    tensor = lax.ppermute(tensor, "col", pairs)
    copies = pl.pallas_call(
        pack_kernel,
        out_shape=shape(rows, HALF, LANES),
        in_specs=[vmem(), vmem()],
        out_specs=vmem(),
        compiler_params=limit(4),
        cost_estimate=pl.CostEstimate(flops=100000000000, bytes_accessed=0, transcendentals=0),
    )(second, scale)
    block = lax.all_to_all(copies, "row", 0, 0, axis_index_groups=[list(PLANE)])
    weights, gram = pl.pallas_call(
        weights_kernel,
        out_shape=(shape(slices, inner, LANES, dtype=BF16), shape(GRAM_ROWS, LANES)),
        in_specs=[vmem(), vmem()],
        out_specs=(vmem(), vmem()),
        compiler_params=limit(8),
        cost_estimate=pl.CostEstimate(flops=0, bytes_accessed=4 << 20, transcendentals=0),
    )(block, scale)
    theirs = pl.pallas_call(
        partner_kernel,
        out_shape=shape(chips * HALF + GRAM_ROWS, LANES),
        in_specs=[vmem(), vmem(), vmem()],
        out_specs=vmem(),
        compiler_params=limit(12),
        cost_estimate=pl.CostEstimate(flops=0, bytes_accessed=4 << 20, transcendentals=0),
    )(tensor, weights, gram)
    got = lax.ppermute(theirs, "col", pairs)
    mine = pl.pallas_call(
        own_kernel,
        out_shape=shape(chips * HALF, LANES),
        in_specs=[vmem(), vmem()],
        out_specs=vmem(),
        compiler_params=limit(12),
        cost_estimate=pl.CostEstimate(flops=0, bytes_accessed=4 << 20, transcendentals=0),
    )(tensor, weights)
    sent = pl.pallas_call(
        join_kernel,
        out_shape=shape(chips, HALF + GRAM_ROWS, LANES),
        in_specs=[vmem(), vmem(), vmem()],
        out_specs=vmem(),
        compiler_params=limit(4),
    )(mine, theirs, got)
    sides = [[2 * chip + core for chip in CHIPS] for core in range(2)]
    total = lax.all_to_all(sent, "col", 0, 0, axis_index_groups=sides)
    return pl.pallas_call(
        solve_kernel,
        out_shape=shape(RANK, RANK),
        in_specs=[vmem()],
        out_specs=vmem(),
        compiler_params=limit(4),
    )(total)


def solution(mesh):
    in_specs = (P(None, "row", "col"), P(("col", "row"), None), P())
    out_specs = P(("row", "col"), None)
    return jax.shard_map(body, mesh=mesh, in_specs=in_specs, out_specs=out_specs, check_vma=False)
```

```python
import jax
import jax.numpy as jnp
from jax import lax
from jax.experimental import pallas as pl
from jax.experimental.pallas import tpu as pltpu
from jax.sharding import PartitionSpec as P

F32 = jnp.float32
BF16 = jnp.bfloat16
RANK = 64
LANES = 128
HALF = 32
STRIP = 8
GROUP = 8
GRAM_ROWS = 24
CHIPS = (5, 6, 4, 7, 0, 3, 1, 2)
PLANE = (10, 11, 12, 13, 14, 15, 0, 1, 2, 3, 4, 5, 6, 7, 8, 9)


def vmem():
    return pl.BlockSpec(memory_space=pltpu.VMEM)


def anywhere():
    return pl.BlockSpec(memory_space=pl.ANY)


def in_hbm(x):
    return pltpu.with_memory_space_constraint(x, pltpu.HBM)


def limit(mib):
    return pltpu.CompilerParams(vmem_limit_bytes=mib << 20)


def shape(*dims, dtype=F32):
    return jax.ShapeDtypeStruct(dims, dtype)


def scale_kernel(third_ref, out_ref):
    slices = third_ref.shape[0]
    out_ref[:slices, :RANK] = third_ref[...]
    out_ref[:slices, RANK:] = third_ref[...]


def pack_kernel(second_ref, scale_ref, out_ref):
    del scale_ref
    packed = jnp.concatenate([second_ref[:HALF, :], second_ref[HALF:, :]], axis=1)
    for peer in range(out_ref.shape[0]):
        out_ref[peer] = packed


def swap(x):
    return pltpu.roll(x, RANK, 1)


def lower_lanes(rows):
    return lax.broadcasted_iota(jnp.int32, (rows, LANES), 1) < RANK


def make_weights(rows_ref, scale_ref, weights):
    left = lower_lanes(HALF)
    for slot, peer in enumerate(PLANE):
        here = rows_ref[slot]
        there = swap(here)
        for k in range(weights.shape[0]):
            a = here * scale_ref[k : k + 1, :]
            b = there * scale_ref[k : k + 1, :]
            a_hi = a.astype(BF16).astype(F32)
            b_hi = b.astype(BF16).astype(F32)
            first = jnp.where(left, a_hi, b - b_hi)
            other = jnp.where(left, b_hi, a - a_hi)
            base = peer * RANK
            weights[k, base : base + HALF, :] = first.astype(BF16)
            weights[k, base + HALF : base + RANK, :] = other.astype(BF16)


def multiply(tensor_ref, weights, out_ref, first, side):
    left = lower_lanes(HALF)
    total = jnp.zeros((GROUP * RANK, LANES), F32)
    for k in range(weights.shape[0]):
        block = jnp.concatenate(
            [
                tensor_ref[k, pl.ds(pl.multiple_of((2 * chip + side) * RANK, RANK), RANK), :]
                for chip in range(first, first + GROUP)
            ],
            axis=0,
        )
        high = block.astype(BF16)
        low = (block - high.astype(F32)).astype(BF16)
        w = weights[k]
        total += jnp.dot(high, w, preferred_element_type=F32)
        total += jnp.dot(low, w, preferred_element_type=F32)
    total += swap(total)
    for s in range(GROUP):
        upper = total[s * RANK : s * RANK + HALF]
        lower = total[s * RANK + HALF : (s + 1) * RANK]
        out_ref[(first + s) * HALF : (first + s + 1) * HALF, :] = jnp.where(left, upper, lower)


def pack_gram(gram):
    quarter = HALF // 4
    top = jnp.concatenate([gram[: HALF // 2], gram[HALF // 2 : HALF]], axis=1)
    corner = [
        gram[HALF + quarter * b : HALF + quarter * (b + 1), HALF:] for b in range(4)
    ]
    return jnp.concatenate([top, jnp.concatenate(corner, axis=1)], axis=0)


def inner_products(a, b):
    return lax.dot_general(a, b, (((0,), (0,)), ((), ())), preferred_element_type=F32)


def own_quarters(x):
    return x[:RANK, :RANK] + x[RANK:, RANK:]


def weights_kernel(rows_ref, scale_ref, weights, gram_ref):
    make_weights(rows_ref, scale_ref, weights)
    flat = rows_ref[...].reshape(-1, LANES)
    high = flat.astype(BF16)
    rest = flat - high.astype(F32)
    middle = rest.astype(BF16)
    low = (rest - middle.astype(F32)).astype(BF16)
    cross = inner_products(high, jnp.concatenate([middle, low], axis=1))
    cross = own_quarters(cross[:, :LANES] + cross[:, LANES:])
    square = own_quarters(inner_products(high, high) + inner_products(middle, middle))
    third = scale_ref[: weights.shape[0], :]
    outer = lax.dot_general(
        third, third, (((0,), (0,)), ((), ())),
        precision=lax.Precision.HIGHEST, preferred_element_type=F32,
    )
    gram = (square + cross + cross.T) * outer[:RANK, :RANK]
    gram_ref[...] = pack_gram(gram)


def partner_kernel(tensor_ref, weights, gram_ref, out_ref):
    core = lax.rem(lax.axis_index("col"), 2)
    for first in range(0, len(CHIPS), GROUP):
        multiply(tensor_ref, weights, out_ref, first, 1 - core)
    out_ref[len(CHIPS) * HALF :, :] = gram_ref[...]


def own_kernel(tensor_ref, weights, out_ref):
    core = lax.rem(lax.axis_index("col"), 2)
    for first in range(0, len(CHIPS), GROUP):
        multiply(tensor_ref, weights, out_ref, first, core)


def join_kernel(own_ref, theirs_ref, got_ref, out_ref):
    chips = out_ref.shape[0]
    gram = theirs_ref[chips * HALF :, :] + got_ref[chips * HALF :, :]
    for chip in range(chips):
        part = slice(chip * HALF, (chip + 1) * HALF)
        slot = CHIPS.index(chip)
        out_ref[slot, :HALF, :] = own_ref[part, :] + got_ref[part, :]
        out_ref[slot, HALF:, :] = gram


def lane(x, c):
    return jnp.broadcast_to(x[:, c : c + 1], (STRIP, LANES))


def pairwise(terms):
    while len(terms) > 1:
        terms = [terms[i] + terms[i + 1] for i in range(0, len(terms), 2)]
    return terms[0]


def eliminate(diag, others, row_id):
    diag = list(diag)
    for j in range(STRIP):
        inv = 1.0 / jnp.broadcast_to(diag[j][j : j + 1, :], (STRIP, LANES))
        ratio = jnp.where(row_id == j, 1.0 - inv, diag[j] * inv)
        for m in range(j + 1, STRIP):
            diag[m] = diag[m] - ratio * diag[m][j : j + 1, :]
        others = [x - ratio * x[j : j + 1, :] for x in others]
    return others


def solve_kernel(got_ref, out_ref):
    total = pairwise([got_ref[peer] for peer in range(got_ref.shape[0])])
    moved = jnp.transpose(jnp.concatenate([total[:HALF]] * 4, axis=0))
    rhs = jnp.concatenate([moved[:RANK, :HALF], moved[RANK:, :HALF]], axis=1)
    top = total[HALF : HALF + HALF // 2]
    corner = total[HALF + HALF // 2 :]
    upper = jnp.concatenate([top[:, :RANK], top[:, RANK:]], axis=0)
    beside = jnp.transpose(upper[:, HALF:])
    below = jnp.concatenate([corner[:, HALF * b : HALF * (b + 1)] for b in range(4)], axis=0)
    lower = jnp.concatenate([beside, below], axis=1)
    system = jnp.concatenate([jnp.concatenate([upper, lower], axis=0), rhs], axis=1)
    strips = RANK // STRIP
    a = [system[STRIP * q : STRIP * (q + 1)] for q in range(strips)]
    row_id = lax.broadcasted_iota(jnp.int32, (STRIP, LANES), 0)
    diag = [lane(a[0], m) for m in range(STRIP)]
    for p in range(strips):
        base = STRIP * p
        cols = [
            [lane(a[q], base + m) for m in range(STRIP)] if q != p else None
            for q in range(strips)
        ]
        ahead = []
        if p + 1 < strips:
            ahead = [lane(a[p], base + STRIP + m) for m in range(STRIP)]
            old = [lane(a[p + 1], base + STRIP + m) for m in range(STRIP)]
        pivot, *ahead = eliminate(diag, [a[p]] + ahead, row_id)
        a[p] = pivot
        if p + 1 < strips:
            diag = [
                old[m]
                - pairwise([cols[p + 1][k] * ahead[m][k : k + 1, :] for k in range(STRIP)])
                for m in range(STRIP)
            ]
        for q in range(strips):
            if q != p:
                a[q] = a[q] - pairwise(
                    [cols[q][m] * pivot[m : m + 1, :] for m in range(STRIP)]
                )
    solved = jnp.concatenate(a, axis=0)
    out_ref[...] = jnp.transpose(jnp.concatenate([solved, solved], axis=0))[RANK:, :RANK]


def body(tensor, second, third):
    rows = lax.axis_size("row")
    cols = lax.axis_size("col")
    chips = cols // 2
    slices, own, inner = tensor.shape
    pairs = [(i, i ^ 1) for i in range(cols)]
    second = lax.ppermute(second, "col", pairs)
    scale = pl.pallas_call(
        scale_kernel,
        out_shape=shape(STRIP, LANES),
        in_specs=[vmem()],
        out_specs=vmem(),
        compiler_params=limit(4),
        cost_estimate=pl.CostEstimate(flops=0, bytes_accessed=4 << 20, transcendentals=0),
    )(third)
    tensor = lax.ppermute(tensor, "col", pairs)
    copies = pl.pallas_call(
        pack_kernel,
        out_shape=shape(rows, HALF, LANES),
        in_specs=[vmem(), vmem()],
        out_specs=vmem(),
        compiler_params=limit(4),
        cost_estimate=pl.CostEstimate(flops=100000000000, bytes_accessed=0, transcendentals=0),
    )(second, scale)
    block = lax.all_to_all(copies, "row", 0, 0, axis_index_groups=[list(PLANE)])
    weights, gram = pl.pallas_call(
        weights_kernel,
        out_shape=(shape(slices, inner, LANES, dtype=BF16), shape(GRAM_ROWS, LANES)),
        in_specs=[vmem(), vmem()],
        out_specs=(vmem(), vmem()),
        compiler_params=limit(8),
        cost_estimate=pl.CostEstimate(flops=0, bytes_accessed=4 << 20, transcendentals=0),
    )(block, scale)
    theirs = pl.pallas_call(
        partner_kernel,
        out_shape=shape(chips * HALF + GRAM_ROWS, LANES),
        in_specs=[vmem(), vmem(), vmem()],
        out_specs=vmem(),
        compiler_params=limit(12),
        cost_estimate=pl.CostEstimate(flops=0, bytes_accessed=4 << 20, transcendentals=0),
    )(tensor, weights, gram)
    got = lax.ppermute(theirs, "col", pairs)
    mine = pl.pallas_call(
        own_kernel,
        out_shape=shape(chips * HALF, LANES),
        in_specs=[vmem(), vmem()],
        out_specs=vmem(),
        compiler_params=limit(12),
        cost_estimate=pl.CostEstimate(flops=0, bytes_accessed=4 << 20, transcendentals=0),
    )(tensor, weights)
    sent = pl.pallas_call(
        join_kernel,
        out_shape=shape(chips, HALF + GRAM_ROWS, LANES),
        in_specs=[vmem(), vmem(), vmem()],
        out_specs=vmem(),
        compiler_params=limit(4),
    )(mine, theirs, got)
    sides = [[2 * chip + core for chip in CHIPS] for core in range(2)]
    total = lax.all_to_all(sent, "col", 0, 0, axis_index_groups=sides)
    return pl.pallas_call(
        solve_kernel,
        out_shape=shape(RANK, RANK),
        in_specs=[vmem()],
        out_specs=vmem(),
        compiler_params=limit(4),
    )(total)


def solution(mesh):
    in_specs = (P(None, "row", "col"), P(("col", "row"), None), P())
    out_specs = P(("row", "col"), None)
    return jax.shard_map(body, mesh=mesh, in_specs=in_specs, out_specs=out_specs, check_vma=False)
```

```python
import jax
import jax.numpy as jnp
from jax import lax
from jax.experimental import pallas as pl
from jax.experimental.pallas import tpu as pltpu
from jax.sharding import PartitionSpec as P

F32 = jnp.float32
BF16 = jnp.bfloat16
RANK = 64
LANES = 128
HALF = 32
STRIP = 8
GROUP = 8
GRAM_ROWS = 24
CHIPS = (5, 6, 4, 7, 0, 3, 1, 2)
PLANE = (10, 11, 12, 13, 14, 15, 0, 1, 2, 3, 4, 5, 6, 7, 8, 9)


def vmem():
    return pl.BlockSpec(memory_space=pltpu.VMEM)


def anywhere():
    return pl.BlockSpec(memory_space=pl.ANY)


def in_hbm(x):
    return pltpu.with_memory_space_constraint(x, pltpu.HBM)


def limit(mib):
    return pltpu.CompilerParams(vmem_limit_bytes=mib << 20)


def shape(*dims, dtype=F32):
    return jax.ShapeDtypeStruct(dims, dtype)


def scale_kernel(third_ref, out_ref):
    slices = third_ref.shape[0]
    out_ref[:slices, :RANK] = third_ref[...]
    out_ref[:slices, RANK:] = third_ref[...]


def pack_kernel(second_ref, scale_ref, out_ref):
    del scale_ref
    packed = jnp.concatenate([second_ref[:HALF, :], second_ref[HALF:, :]], axis=1)
    for peer in range(out_ref.shape[0]):
        out_ref[peer] = packed


def swap(x):
    return pltpu.roll(x, RANK, 1)


def lower_lanes(rows):
    return lax.broadcasted_iota(jnp.int32, (rows, LANES), 1) < RANK


def make_weights(rows_ref, scale_ref, weights):
    left = lower_lanes(HALF)
    for slot, peer in enumerate(PLANE):
        here = rows_ref[slot]
        there = swap(here)
        for k in range(weights.shape[0]):
            a = here * scale_ref[k : k + 1, :]
            b = there * scale_ref[k : k + 1, :]
            a_hi = a.astype(BF16).astype(F32)
            b_hi = b.astype(BF16).astype(F32)
            first = jnp.where(left, a_hi, b - b_hi)
            other = jnp.where(left, b_hi, a - a_hi)
            base = peer * RANK
            weights[k, base : base + HALF, :] = first.astype(BF16)
            weights[k, base + HALF : base + RANK, :] = other.astype(BF16)


def multiply(tensor_ref, weights, out_ref, first, side):
    left = lower_lanes(HALF)
    total = jnp.zeros((GROUP * RANK, LANES), F32)
    for k in range(weights.shape[0]):
        block = jnp.concatenate(
            [
                tensor_ref[k, pl.ds(pl.multiple_of((2 * chip + side) * RANK, RANK), RANK), :]
                for chip in range(first, first + GROUP)
            ],
            axis=0,
        )
        high = block.astype(BF16)
        low = (block - high.astype(F32)).astype(BF16)
        w = weights[k]
        total += jnp.dot(high, w, preferred_element_type=F32)
        total += jnp.dot(low, w, preferred_element_type=F32)
    total += swap(total)
    for s in range(GROUP):
        upper = total[s * RANK : s * RANK + HALF]
        lower = total[s * RANK + HALF : (s + 1) * RANK]
        out_ref[(first + s) * HALF : (first + s + 1) * HALF, :] = jnp.where(left, upper, lower)


def pack_gram(gram):
    quarter = HALF // 4
    top = jnp.concatenate([gram[: HALF // 2], gram[HALF // 2 : HALF]], axis=1)
    corner = [
        gram[HALF + quarter * b : HALF + quarter * (b + 1), HALF:] for b in range(4)
    ]
    return jnp.concatenate([top, jnp.concatenate(corner, axis=1)], axis=0)


def inner_products(a, b):
    return lax.dot_general(a, b, (((0,), (0,)), ((), ())), preferred_element_type=F32)


def own_quarters(x):
    return x[:RANK, :RANK] + x[RANK:, RANK:]


def weights_kernel(rows_ref, scale_ref, weights, gram_ref):
    make_weights(rows_ref, scale_ref, weights)
    flat = rows_ref[...].reshape(-1, LANES)
    high = flat.astype(BF16)
    rest = flat - high.astype(F32)
    middle = rest.astype(BF16)
    low = (rest - middle.astype(F32)).astype(BF16)
    cross = inner_products(high, jnp.concatenate([middle, low], axis=1))
    cross = own_quarters(cross[:, :LANES] + cross[:, LANES:])
    square = own_quarters(inner_products(high, high) + inner_products(middle, middle))
    third = scale_ref[: weights.shape[0], :]
    outer = lax.dot_general(
        third, third, (((0,), (0,)), ((), ())),
        precision=lax.Precision.HIGHEST, preferred_element_type=F32,
    )
    gram = (square + cross + cross.T) * outer[:RANK, :RANK]
    gram_ref[...] = pack_gram(gram)


def partner_kernel(tensor_ref, weights, gram_ref, out_ref):
    core = lax.rem(lax.axis_index("col"), 2)
    for first in range(0, len(CHIPS), GROUP):
        multiply(tensor_ref, weights, out_ref, first, 1 - core)
    out_ref[len(CHIPS) * HALF :, :] = gram_ref[...]


def own_kernel(tensor_ref, weights, out_ref):
    core = lax.rem(lax.axis_index("col"), 2)
    for first in range(0, len(CHIPS), GROUP):
        multiply(tensor_ref, weights, out_ref, first, core)


def join_kernel(own_ref, theirs_ref, got_ref, out_ref):
    chips = out_ref.shape[0]
    gram = theirs_ref[chips * HALF :, :] + got_ref[chips * HALF :, :]
    for chip in range(chips):
        part = slice(chip * HALF, (chip + 1) * HALF)
        slot = CHIPS.index(chip)
        out_ref[slot, :HALF, :] = own_ref[part, :] + got_ref[part, :]
        out_ref[slot, HALF:, :] = gram


def row(x, r):
    return jnp.broadcast_to(x[r : r + 1, :], (STRIP, LANES))


def lane(x, c):
    return jnp.broadcast_to(x[:, c : c + 1], (STRIP, LANES))


def pairwise(terms):
    while len(terms) > 1:
        terms = [terms[i] + terms[i + 1] for i in range(0, len(terms), 2)]
    return terms[0]


def eliminate(diag, others, row_id):
    diag = list(diag)
    pivot = row(diag[0], 0)
    for j in range(STRIP):
        inv = 1.0 / pivot
        if j + 1 < STRIP:
            corner = row(diag[j], j + 1) * row(diag[j + 1], j)
            pivot = row(diag[j + 1], j + 1) - corner * inv
        ratio = jnp.where(row_id == j, 1.0 - inv, diag[j] * inv)
        for m in range(j + 1, STRIP):
            diag[m] = diag[m] - ratio * diag[m][j : j + 1, :]
        others = [x - ratio * x[j : j + 1, :] for x in others]
    return others


def solve_kernel(got_ref, out_ref):
    total = pairwise([got_ref[peer] for peer in range(got_ref.shape[0])])
    moved = jnp.transpose(jnp.concatenate([total[:HALF]] * 4, axis=0))
    rhs = jnp.concatenate([moved[:RANK, :HALF], moved[RANK:, :HALF]], axis=1)
    top = total[HALF : HALF + HALF // 2]
    corner = total[HALF + HALF // 2 :]
    upper = jnp.concatenate([top[:, :RANK], top[:, RANK:]], axis=0)
    beside = jnp.transpose(upper[:, HALF:])
    below = jnp.concatenate([corner[:, HALF * b : HALF * (b + 1)] for b in range(4)], axis=0)
    lower = jnp.concatenate([beside, below], axis=1)
    system = jnp.concatenate([jnp.concatenate([upper, lower], axis=0), rhs], axis=1)
    strips = RANK // STRIP
    a = [system[STRIP * q : STRIP * (q + 1)] for q in range(strips)]
    row_id = lax.broadcasted_iota(jnp.int32, (STRIP, LANES), 0)
    diag = [lane(a[0], m) for m in range(STRIP)]
    for p in range(strips):
        base = STRIP * p
        cols = [
            [lane(a[q], base + m) for m in range(STRIP)] if q != p else None
            for q in range(strips)
        ]
        ahead = []
        if p + 1 < strips:
            ahead = [lane(a[p], base + STRIP + m) for m in range(STRIP)]
            old = [lane(a[p + 1], base + STRIP + m) for m in range(STRIP)]
        pivot, *ahead = eliminate(diag, [a[p]] + ahead, row_id)
        a[p] = pivot
        if p + 1 < strips:
            diag = [
                old[m]
                - pairwise([cols[p + 1][k] * ahead[m][k : k + 1, :] for k in range(STRIP)])
                for m in range(STRIP)
            ]
        spread = [row(pivot, m) for m in range(STRIP)]
        for q in range(strips):
            if q != p:
                a[q] = a[q] - pairwise([cols[q][m] * spread[m] for m in range(STRIP)])
    solved = jnp.concatenate(a, axis=0)
    out_ref[...] = jnp.transpose(jnp.concatenate([solved, solved], axis=0))[RANK:, :RANK]


def body(tensor, second, third):
    rows = lax.axis_size("row")
    cols = lax.axis_size("col")
    chips = cols // 2
    slices, own, inner = tensor.shape
    pairs = [(i, i ^ 1) for i in range(cols)]
    second = lax.ppermute(second, "col", pairs)
    scale = pl.pallas_call(
        scale_kernel,
        out_shape=shape(STRIP, LANES),
        in_specs=[vmem()],
        out_specs=vmem(),
        compiler_params=limit(4),
        cost_estimate=pl.CostEstimate(flops=0, bytes_accessed=4 << 20, transcendentals=0),
    )(third)
    tensor = lax.ppermute(tensor, "col", pairs)
    copies = pl.pallas_call(
        pack_kernel,
        out_shape=shape(rows, HALF, LANES),
        in_specs=[vmem(), vmem()],
        out_specs=vmem(),
        compiler_params=limit(4),
        cost_estimate=pl.CostEstimate(flops=100000000000, bytes_accessed=0, transcendentals=0),
    )(second, scale)
    block = lax.all_to_all(copies, "row", 0, 0, axis_index_groups=[list(PLANE)])
    weights, gram = pl.pallas_call(
        weights_kernel,
        out_shape=(shape(slices, inner, LANES, dtype=BF16), shape(GRAM_ROWS, LANES)),
        in_specs=[vmem(), vmem()],
        out_specs=(vmem(), vmem()),
        compiler_params=limit(8),
        cost_estimate=pl.CostEstimate(flops=0, bytes_accessed=4 << 20, transcendentals=0),
    )(block, scale)
    theirs = pl.pallas_call(
        partner_kernel,
        out_shape=shape(chips * HALF + GRAM_ROWS, LANES),
        in_specs=[vmem(), vmem(), vmem()],
        out_specs=vmem(),
        compiler_params=limit(12),
        cost_estimate=pl.CostEstimate(flops=0, bytes_accessed=4 << 20, transcendentals=0),
    )(tensor, weights, gram)
    got = lax.ppermute(theirs, "col", pairs)
    mine = pl.pallas_call(
        own_kernel,
        out_shape=shape(chips * HALF, LANES),
        in_specs=[vmem(), vmem()],
        out_specs=vmem(),
        compiler_params=limit(12),
        cost_estimate=pl.CostEstimate(flops=0, bytes_accessed=4 << 20, transcendentals=0),
    )(tensor, weights)
    sent = pl.pallas_call(
        join_kernel,
        out_shape=shape(chips, HALF + GRAM_ROWS, LANES),
        in_specs=[vmem(), vmem(), vmem()],
        out_specs=vmem(),
        compiler_params=limit(4),
    )(mine, theirs, got)
    sides = [[2 * chip + core for chip in CHIPS] for core in range(2)]
    total = lax.all_to_all(sent, "col", 0, 0, axis_index_groups=sides)
    return pl.pallas_call(
        solve_kernel,
        out_shape=shape(RANK, RANK),
        in_specs=[vmem()],
        out_specs=vmem(),
        compiler_params=limit(4),
    )(total)


def solution(mesh):
    in_specs = (P(None, "row", "col"), P(("col", "row"), None), P())
    out_specs = P(("row", "col"), None)
    return jax.shard_map(body, mesh=mesh, in_specs=in_specs, out_specs=out_specs, check_vma=False)
```

```python
import jax
import jax.numpy as jnp
from jax import lax
from jax.experimental import pallas as pl
from jax.experimental.pallas import tpu as pltpu
from jax.sharding import PartitionSpec as P

F32 = jnp.float32
BF16 = jnp.bfloat16
RANK = 64
LANES = 128
HALF = 32
STRIP = 8
GROUP = 8
GRAM_ROWS = 24
CHIPS = (5, 4, 6, 7, 0, 3, 1, 2)
PLANE = (10, 11, 12, 13, 14, 15, 0, 1, 2, 3, 4, 5, 6, 7, 8, 9)


def vmem():
    return pl.BlockSpec(memory_space=pltpu.VMEM)


def anywhere():
    return pl.BlockSpec(memory_space=pl.ANY)


def in_hbm(x):
    return pltpu.with_memory_space_constraint(x, pltpu.HBM)


def limit(mib):
    return pltpu.CompilerParams(vmem_limit_bytes=mib << 20)


def shape(*dims, dtype=F32):
    return jax.ShapeDtypeStruct(dims, dtype)


def scale_kernel(third_ref, out_ref):
    slices = third_ref.shape[0]
    out_ref[:slices, :RANK] = third_ref[...]
    out_ref[:slices, RANK:] = third_ref[...]


def pack_kernel(second_ref, scale_ref, out_ref):
    del scale_ref
    packed = jnp.concatenate([second_ref[:HALF, :], second_ref[HALF:, :]], axis=1)
    for peer in range(out_ref.shape[0]):
        out_ref[peer] = packed


def swap(x):
    return pltpu.roll(x, RANK, 1)


def lower_lanes(rows):
    return lax.broadcasted_iota(jnp.int32, (rows, LANES), 1) < RANK


def make_weights(rows_ref, scale_ref, weights):
    left = lower_lanes(HALF)
    for slot, peer in enumerate(PLANE):
        here = rows_ref[slot]
        there = swap(here)
        for k in range(weights.shape[0]):
            a = here * scale_ref[k : k + 1, :]
            b = there * scale_ref[k : k + 1, :]
            a_hi = a.astype(BF16).astype(F32)
            b_hi = b.astype(BF16).astype(F32)
            first = jnp.where(left, a_hi, b - b_hi)
            other = jnp.where(left, b_hi, a - a_hi)
            base = peer * RANK
            weights[k, base : base + HALF, :] = first.astype(BF16)
            weights[k, base + HALF : base + RANK, :] = other.astype(BF16)


def multiply(tensor_ref, weights, out_ref, first, side):
    left = lower_lanes(HALF)
    total = jnp.zeros((GROUP * RANK, LANES), F32)
    for k in range(weights.shape[0]):
        block = jnp.concatenate(
            [
                tensor_ref[k, pl.ds(pl.multiple_of((2 * chip + side) * RANK, RANK), RANK), :]
                for chip in range(first, first + GROUP)
            ],
            axis=0,
        )
        high = block.astype(BF16)
        low = (block - high.astype(F32)).astype(BF16)
        w = weights[k]
        total += jnp.dot(high, w, preferred_element_type=F32)
        total += jnp.dot(low, w, preferred_element_type=F32)
    total += swap(total)
    for s in range(GROUP):
        upper = total[s * RANK : s * RANK + HALF]
        lower = total[s * RANK + HALF : (s + 1) * RANK]
        out_ref[(first + s) * HALF : (first + s + 1) * HALF, :] = jnp.where(left, upper, lower)


def pack_gram(gram):
    quarter = HALF // 4
    top = jnp.concatenate([gram[: HALF // 2], gram[HALF // 2 : HALF]], axis=1)
    corner = [
        gram[HALF + quarter * b : HALF + quarter * (b + 1), HALF:] for b in range(4)
    ]
    return jnp.concatenate([top, jnp.concatenate(corner, axis=1)], axis=0)


def inner_products(a, b):
    return lax.dot_general(a, b, (((0,), (0,)), ((), ())), preferred_element_type=F32)


def own_quarters(x):
    return x[:RANK, :RANK] + x[RANK:, RANK:]


def weights_kernel(rows_ref, scale_ref, weights, gram_ref):
    make_weights(rows_ref, scale_ref, weights)
    flat = rows_ref[...].reshape(-1, LANES)
    high = flat.astype(BF16)
    rest = flat - high.astype(F32)
    middle = rest.astype(BF16)
    low = (rest - middle.astype(F32)).astype(BF16)
    cross = inner_products(high, jnp.concatenate([middle, low], axis=1))
    cross = own_quarters(cross[:, :LANES] + cross[:, LANES:])
    square = own_quarters(inner_products(high, high) + inner_products(middle, middle))
    third = scale_ref[: weights.shape[0], :]
    outer = lax.dot_general(
        third, third, (((0,), (0,)), ((), ())),
        precision=lax.Precision.HIGHEST, preferred_element_type=F32,
    )
    gram = (square + cross + cross.T) * outer[:RANK, :RANK]
    gram_ref[...] = pack_gram(gram)


def partner_kernel(tensor_ref, weights, gram_ref, out_ref):
    core = lax.rem(lax.axis_index("col"), 2)
    for first in range(0, len(CHIPS), GROUP):
        multiply(tensor_ref, weights, out_ref, first, 1 - core)
    out_ref[len(CHIPS) * HALF :, :] = gram_ref[...]


def own_kernel(tensor_ref, weights, out_ref):
    core = lax.rem(lax.axis_index("col"), 2)
    for first in range(0, len(CHIPS), GROUP):
        multiply(tensor_ref, weights, out_ref, first, core)


def join_kernel(own_ref, theirs_ref, got_ref, out_ref):
    chips = out_ref.shape[0]
    gram = theirs_ref[chips * HALF :, :] + got_ref[chips * HALF :, :]
    for chip in range(chips):
        part = slice(chip * HALF, (chip + 1) * HALF)
        slot = CHIPS.index(chip)
        out_ref[slot, :HALF, :] = own_ref[part, :] + got_ref[part, :]
        out_ref[slot, HALF:, :] = gram


def lane(x, c):
    return jnp.broadcast_to(x[:, c : c + 1], (STRIP, LANES))


def pairwise(terms):
    while len(terms) > 1:
        terms = [terms[i] + terms[i + 1] for i in range(0, len(terms), 2)]
    return terms[0]


def eliminate(diag, others, row_id):
    diag = list(diag)
    for j in range(STRIP):
        inv = 1.0 / jnp.broadcast_to(diag[j][j : j + 1, :], (STRIP, LANES))
        ratio = jnp.where(row_id == j, 1.0 - inv, diag[j] * inv)
        for m in range(j + 1, STRIP):
            diag[m] = diag[m] - ratio * diag[m][j : j + 1, :]
        others = [x - ratio * x[j : j + 1, :] for x in others]
    return others


def solve_kernel(got_ref, out_ref):
    total = pairwise([got_ref[peer] for peer in range(got_ref.shape[0])])
    moved = jnp.transpose(jnp.concatenate([total[:HALF]] * 4, axis=0))
    rhs = jnp.concatenate([moved[:RANK, :HALF], moved[RANK:, :HALF]], axis=1)
    top = total[HALF : HALF + HALF // 2]
    corner = total[HALF + HALF // 2 :]
    upper = jnp.concatenate([top[:, :RANK], top[:, RANK:]], axis=0)
    beside = jnp.transpose(upper[:, HALF:])
    below = jnp.concatenate([corner[:, HALF * b : HALF * (b + 1)] for b in range(4)], axis=0)
    lower = jnp.concatenate([beside, below], axis=1)
    system = jnp.concatenate([jnp.concatenate([upper, lower], axis=0), rhs], axis=1)
    strips = RANK // STRIP
    a = [system[STRIP * q : STRIP * (q + 1)] for q in range(strips)]
    row_id = lax.broadcasted_iota(jnp.int32, (STRIP, LANES), 0)
    diag = [lane(a[0], m) for m in range(STRIP)]
    for p in range(strips):
        base = STRIP * p
        cols = [
            [lane(a[q], base + m) for m in range(STRIP)] if q != p else None
            for q in range(strips)
        ]
        ahead = []
        if p + 1 < strips:
            ahead = [lane(a[p], base + STRIP + m) for m in range(STRIP)]
            old = [lane(a[p + 1], base + STRIP + m) for m in range(STRIP)]
        pivot, *ahead = eliminate(diag, [a[p]] + ahead, row_id)
        a[p] = pivot
        if p + 1 < strips:
            diag = [
                old[m]
                - pairwise([cols[p + 1][k] * ahead[m][k : k + 1, :] for k in range(STRIP)])
                for m in range(STRIP)
            ]
        for q in range(strips):
            if q != p:
                a[q] = a[q] - pairwise(
                    [cols[q][m] * pivot[m : m + 1, :] for m in range(STRIP)]
                )
    solved = jnp.concatenate(a, axis=0)
    out_ref[...] = jnp.transpose(jnp.concatenate([solved, solved], axis=0))[RANK:, :RANK]


def body(tensor, second, third):
    rows = lax.axis_size("row")
    cols = lax.axis_size("col")
    chips = cols // 2
    slices, own, inner = tensor.shape
    pairs = [(i, i ^ 1) for i in range(cols)]
    second = lax.ppermute(second, "col", pairs)
    scale = pl.pallas_call(
        scale_kernel,
        out_shape=shape(STRIP, LANES),
        in_specs=[vmem()],
        out_specs=vmem(),
        compiler_params=limit(4),
        cost_estimate=pl.CostEstimate(flops=0, bytes_accessed=4 << 20, transcendentals=0),
    )(third)
    tensor = lax.ppermute(tensor, "col", pairs)
    copies = pl.pallas_call(
        pack_kernel,
        out_shape=shape(rows, HALF, LANES),
        in_specs=[vmem(), vmem()],
        out_specs=vmem(),
        compiler_params=limit(4),
        cost_estimate=pl.CostEstimate(flops=100000000000, bytes_accessed=0, transcendentals=0),
    )(second, scale)
    block = lax.all_to_all(copies, "row", 0, 0, axis_index_groups=[list(PLANE)])
    weights, gram = pl.pallas_call(
        weights_kernel,
        out_shape=(shape(slices, inner, LANES, dtype=BF16), shape(GRAM_ROWS, LANES)),
        in_specs=[vmem(), vmem()],
        out_specs=(vmem(), vmem()),
        compiler_params=limit(8),
        cost_estimate=pl.CostEstimate(flops=0, bytes_accessed=4 << 20, transcendentals=0),
    )(block, scale)
    theirs = pl.pallas_call(
        partner_kernel,
        out_shape=shape(chips * HALF + GRAM_ROWS, LANES),
        in_specs=[vmem(), vmem(), vmem()],
        out_specs=vmem(),
        compiler_params=limit(12),
        cost_estimate=pl.CostEstimate(flops=0, bytes_accessed=4 << 20, transcendentals=0),
    )(tensor, weights, gram)
    got = lax.ppermute(theirs, "col", pairs)
    mine = pl.pallas_call(
        own_kernel,
        out_shape=shape(chips * HALF, LANES),
        in_specs=[vmem(), vmem()],
        out_specs=vmem(),
        compiler_params=limit(12),
        cost_estimate=pl.CostEstimate(flops=0, bytes_accessed=4 << 20, transcendentals=0),
    )(tensor, weights)
    sent = pl.pallas_call(
        join_kernel,
        out_shape=shape(chips, HALF + GRAM_ROWS, LANES),
        in_specs=[vmem(), vmem(), vmem()],
        out_specs=vmem(),
        compiler_params=limit(4),
    )(mine, theirs, got)
    sides = [[2 * chip + core for chip in CHIPS] for core in range(2)]
    total = lax.all_to_all(sent, "col", 0, 0, axis_index_groups=sides)
    return pl.pallas_call(
        solve_kernel,
        out_shape=shape(RANK, RANK),
        in_specs=[vmem()],
        out_specs=vmem(),
        compiler_params=limit(4),
    )(total)


def solution(mesh):
    in_specs = (P(None, "row", "col"), P(("col", "row"), None), P())
    out_specs = P(("row", "col"), None)
    return jax.shard_map(body, mesh=mesh, in_specs=in_specs, out_specs=out_specs, check_vma=False)
```
